256 devices in a mesh: blk: 8 (over y_hi, x), branch: 32 (over z, y_lo, core).
Axes of the slice: x: 4, y: 4 (y_hi: 2, y_lo: 2; y = y_hi * 2 + y_lo), z: 8, core: 2. Of those that a mesh axis runs over, the one named last changes fastest.
Arguments:
- counts: int32 [2048, 16384], P('blk', 'branch'), may hold values from 0 to 192, as said below
- totals: int32 [2048], P('blk'), may hold values from 1 to 3145728, as said below
- lengths: int32 [16384], P('branch'), may hold values from 1 to 999
Outputs:
- distances: float32 [2048, 2048], P('blk')
The draws below stay inside these ranges and needn't reach their ends.
Inputs may be any that keep to these rules, and one draw needn't show every extreme that they name: `counts`: counts_ik is the whole number of reads of sample i below branch k. `totals`: totals_i equals the sum of counts_ik over all 16384 branches.
All inputs are finite; a program needn't handle non-finite values.
Results may differ from the reference program's by a relative error of at most 0.00002.
Values sent between devices are 32-bit elements; how exact they have to be, the bound alone decides.
No kernel may reach another device: no remote copies, remote signals or barrier semaphores. Data moves between devices by JAX's collectives and lax.ppermute only.
A program may use at most 64 MiB of HBM per device.

```python
from functools import partial
import jax
import jax.numpy as jnp
from jax import lax

SAMPLES = 2048
BRANCHES = 16384


def sample_row(key, sample_index):
    clade_len = 32
    clade_count = BRANCHES // clade_len
    presence = jax.random.randint(jax.random.fold_in(key, 11), (6, clade_count), 0, 5)
    row_key = jax.random.fold_in(jax.random.fold_in(key, 13), sample_index)
    community = jax.random.randint(jax.random.fold_in(row_key, 1), (), 0, 6)
    clade_index = jnp.arange(clade_count, dtype=jnp.int32)
    own_presence = jnp.take(presence, community, axis=0)
    clade_on = (own_presence >= 2) | (clade_index % 6 == community)
    exponent = jax.random.randint(jax.random.fold_in(row_key, 2), (clade_count,), 0, 7)
    clade_level = jnp.left_shift(jnp.ones((clade_count,), jnp.int32), exponent)
    clade_amount = jnp.where(clade_on, clade_level, jnp.zeros((clade_count,), jnp.int32))
    leaf_index = jnp.arange(clade_len, dtype=jnp.int32)
    leaf_draw = jax.random.randint(jax.random.fold_in(row_key, 3), (clade_count, clade_len), 0, 4)
    leaf_on = ((leaf_draw > 0) | (leaf_index[None, :] == 0)).astype(jnp.int32)
    leaf_amount = jax.random.randint(jax.random.fold_in(row_key, 4), (clade_count, clade_len), 1, 4)
    drawn = (clade_amount[:, None] * leaf_on * leaf_amount).reshape(BRANCHES).astype(jnp.int32)
    fullest = jnp.full((BRANCHES,), 192, jnp.int32)
    return jnp.where(sample_index == 0, fullest, drawn)


def draw_counts(key, part):
    return lax.map(partial(sample_row, key), jnp.arange(SAMPLES, dtype=jnp.int32))


def draw_totals(key, part):

    def row_total(sample_index):
        return jnp.sum(sample_row(key, sample_index)).astype(jnp.int32)
    return lax.map(row_total, jnp.arange(SAMPLES, dtype=jnp.int32))


def plant(values, rng, least, top_value):
    longest = values.shape.index(max(values.shape))
    spots = []
    for shift in (0, 1):
        where = [jax.random.randint(jax.random.fold_in(rng, axis), (), 0, length) for axis, length in enumerate(values.shape)]
        where[longest] = (where[longest] + shift) % values.shape[longest]
        spots.append(tuple(where))
    return values.at[spots[0]].set(least).at[spots[1]].set(top_value)


def setup_inputs(seed: int = 0) -> dict:
    streams_of = jax.random.split(jax.random.key(seed), 4)
    return {
        "counts": draw_counts(jax.random.fold_in(streams_of[3], 71), 0),
        "totals": draw_totals(jax.random.fold_in(streams_of[3], 71), 0),
        "lengths": plant(jax.random.randint(streams_of[2], (BRANCHES,), 1, 1000), jax.random.fold_in(streams_of[2], 1), 1, 999).astype(jnp.int32),
    }


def reference(counts, totals, lengths):
    scaled = lengths.astype(jnp.float32) * 0.001
    widened = scaled[None, :] * counts.astype(jnp.float32) / totals.astype(jnp.float32)[:, None]
    mass = jnp.sum(widened, axis=1)

    def one_row(vector):
        return jnp.sum(jnp.abs(vector[None, :] - widened), axis=1)

    spread = lax.map(one_row, widened)
    return spread / (mass[:, None] + mass[None, :])
```

```python
import jax
import jax.numpy as jnp
from jax import lax
from jax.experimental import pallas as pl
from jax.experimental.pallas import tpu as pltpu
from jax.sharding import PartitionSpec as P

F32 = jnp.float32
ROWS = 256
KS = 512
BLOCKS = 8
SLOTS = 5
WIDTH = SLOTS * ROWS


def block_at(y, x):
    return (y % 2) * 4 + x % 4


def partner_tables():
    first, second, third, fourth = [], [], [], []
    for b in range(BLOCKS):
        y, x = b // 4, b % 4
        first.append(block_at(y, x + 1))
        second.append(block_at(y + 1, x + 1))
        cycle = {(0, 0): (0, 2), (0, 1): (1, 2), (1, 1): (1, 0), (1, 0): (0, 0)}
        ny, nx = cycle[(y, x // 2)]
        third.append(block_at(ny, nx + x % 2))
        fourth.append(block_at(y + 1, x + 2))
    return [first, second, third, fourth]


PARTNERS = partner_tables()
OWNERS = [[table.index(b) for b in range(BLOCKS)] for table in PARTNERS[:3]]


def params():
    return pltpu.CompilerParams(vmem_limit_bytes=56 << 20)


def weigh_kernel(counts_ref, totals_ref, lengths_ref, w_ref, wt_ref):
    scaled = lengths_ref[...].astype(F32) * 0.001
    weighted = scaled * counts_ref[...].astype(F32) / totals_ref[...].astype(F32)
    w_ref[...] = weighted
    wt_ref[...] = weighted.T


def weigh(counts, totals, lengths):
    return pl.pallas_call(
        weigh_kernel,
        out_shape=(
            jax.ShapeDtypeStruct((ROWS, KS), F32),
            jax.ShapeDtypeStruct((KS, ROWS), F32),
        ),
        compiler_params=params(),
        name="weigh",
    )(counts, totals.reshape(ROWS, 1), lengths.reshape(1, KS))


def spread_kernel(w_ref, t0, t1, t2, t3, t4, out_ref, rows_ref, mass_ref, col_ref):
    group = 32
    lanes = WIDTH // 128
    blocks = [t0, t1, t2, t3, t4]

    def fill(k8, masses):
        at = pl.ds(pl.multiple_of(k8 * 8, 8), 8)
        rows = [ref[at, :] for ref in blocks]
        for s in range(8):
            spans = [jnp.broadcast_to(r[s : s + 1], (8, ROWS)) for r in rows]
            for n in range(SLOTS):
                rows_ref[k8 * 8 + s, :, n * ROWS : (n + 1) * ROWS] = spans[n]
            masses = tuple(m + v for m, v in zip(masses, spans, strict=True))
        return masses

    zero = jnp.zeros((8, ROWS), F32)
    masses = lax.fori_loop(0, KS // 8, fill, (zero,) * SLOTS)
    for n in range(SLOTS):
        mass_ref[:, n * ROWS : (n + 1) * ROWS] = masses[n]
    for h in range(2):
        span = mass_ref[0:1, h * 128 : (h + 1) * 128]
        col_ref[h * 128 : (h + 1) * 128, :] = jnp.broadcast_to(span, (128, 128)).T
    for h in range(2):
        out_ref[h, 128:136, :] = mass_ref[...]

    def tile(t, carry):
        i0 = pl.multiple_of(t * group, group)

        def chunk(c, acc):
            k0 = pl.multiple_of(c * 128, 128)
            a = w_ref[pl.ds(i0, group), pl.ds(k0, 128)]
            for kk in range(128):
                cols = [
                    jnp.broadcast_to(a[8 * r : 8 * r + 8, kk : kk + 1], (8, 128))
                    for r in range(group // 8)
                ]
                spans = [rows_ref[k0 + kk, :, 128 * j : 128 * j + 128] for j in range(lanes)]
                acc = tuple(
                    acc[r * lanes + j] + jnp.minimum(cols[r], spans[j])
                    for r in range(group // 8)
                    for j in range(lanes)
                )
            return acc

        start = (jnp.zeros((8, 128), F32),) * (group // 8 * lanes)
        acc = lax.fori_loop(0, KS // 128, chunk, start)
        half = t // 4
        r0 = pl.multiple_of((t % 4) * group, group)
        for r in range(group // 8):
            own = col_ref[pl.ds(i0 + 8 * r, 8), :]
            for j in range(lanes):
                both = own + mass_ref[:, 128 * j : 128 * j + 128]
                out_ref[half, pl.ds(r0 + 8 * r, 8), 128 * j : 128 * j + 128] = (
                    both - 2.0 * acc[r * lanes + j]
                )
        return carry

    lax.fori_loop(0, ROWS // group, tile, 0)


def spread(w, blocks):
    return pl.pallas_call(
        spread_kernel,
        out_shape=jax.ShapeDtypeStruct((2, 136, WIDTH), F32),
        scratch_shapes=[
            pltpu.VMEM((KS, 8, WIDTH), F32),
            pltpu.VMEM((8, WIDTH), F32),
            pltpu.VMEM((ROWS, 128), F32),
        ],
        compiler_params=params(),
        name="spread",
    )(w, *blocks)


def assemble_kernel(where_ref, own_ref, other_ref, out_ref, all_ref):
    core, z = where_ref[0], where_ref[1]
    for ref, c in ((own_ref, core), (other_ref, 1 - core)):
        for d in range(8):
            for y in range(2):
                row = c * 128 + y * 64 + ((z - d + 8) % 8) * 8
                at = pl.ds(pl.multiple_of(row, 8), 8)
                all_ref[at, :] = ref[d, y]
    for n in range(8):
        to = pl.ds(pl.multiple_of(where_ref[2 + n] * ROWS, ROWS), ROWS)
        part = all_ref[:, n * ROWS : (n + 1) * ROWS]
        out_ref[:, to] = part if n < SLOTS else part.T


def assemble(where, own, other):
    return pl.pallas_call(
        assemble_kernel,
        out_shape=jax.ShapeDtypeStruct((ROWS, BLOCKS * ROWS), F32),
        in_specs=[
            pl.BlockSpec(memory_space=pltpu.SMEM),
            pl.BlockSpec(memory_space=pltpu.VMEM),
            pl.BlockSpec(memory_space=pltpu.VMEM),
        ],
        out_specs=pl.BlockSpec(memory_space=pltpu.VMEM),
        scratch_shapes=[pltpu.VMEM((ROWS, BLOCKS * ROWS), F32)],
        compiler_params=params(),
        name="assemble",
    )(where, own, other)


def on_device(counts, totals, lengths):
    blk = lax.axis_index("blk")
    branch = lax.axis_index("branch")
    core, ylo, z = branch % 2, (branch // 2) % 2, branch // 4

    w, wt = weigh(counts, totals, lengths)
    blocks = [wt]
    for table in PARTNERS:
        blocks.append(lax.ppermute(wt, "blk", [(table[b], b) for b in range(BLOCKS)]))
    parts = spread(w, blocks)

    def over_branch(v, move):
        return lax.ppermute(v, "branch", [(i, move(i)) for i in range(32)])

    keep = lax.dynamic_index_in_dim(parts, core, 0, False)
    send = lax.dynamic_index_in_dim(parts, 1 - core, 0, False)
    parts = keep + over_branch(send, lambda i: i ^ 1)
    rows = parts[:128].reshape(2, 64, WIDTH)
    mass = parts[128:]
    keep = lax.dynamic_index_in_dim(rows, ylo, 0, False)
    send = lax.dynamic_index_in_dim(rows, 1 - ylo, 0, False)
    parts = jnp.concatenate([keep, mass]) + over_branch(
        jnp.concatenate([send, mass]), lambda i: i ^ 2
    )
    rows = parts[:64].reshape(8, 8, WIDTH)
    mass = jnp.pad(parts[64].reshape(8, WIDTH // 8), ((0, 0), (0, 256 - WIDTH // 8)))
    mass = jnp.broadcast_to(mass[None], (8, 8, 256))
    groups = [[zz * 4 + r for zz in range(8)] for r in range(4)]
    shards = lax.all_to_all(
        jnp.concatenate([rows, mass], axis=2), "branch", 0, 0, axis_index_groups=groups
    )
    shard = jnp.sum(shards, axis=0)
    mass = shard[:, WIDTH : WIDTH + WIDTH // 8].reshape(WIDTH)
    own = lax.dynamic_slice_in_dim(mass, core * 128 + ylo * 64 + z * 8, 8)
    dist = shard[:, :WIDTH] / (own[:, None] + mass[None, :])

    pieces = [dist]
    for n in range(3):
        piece = dist[:, (n + 1) * ROWS : (n + 2) * ROWS]
        route = [(b, PARTNERS[n][b]) for b in range(BLOCKS)]
        pieces.append(lax.ppermute(piece, "blk", route))
    mine = jnp.concatenate(pieces, axis=1)
    theirs = over_branch(mine, lambda i: i ^ 2)
    pair = jnp.where(ylo == 0, jnp.stack([mine, theirs]), jnp.stack([theirs, mine]))
    around = [pair]
    for d in range(1, 8):
        around.append(over_branch(pair, lambda i, d=d: (i + 4 * d) % 32))
    around = jnp.stack(around)
    other = over_branch(around, lambda i: i ^ 1)

    tables = jnp.array(PARTNERS + OWNERS, jnp.int32)
    cols = lax.dynamic_index_in_dim(tables, blk, 1, False)
    where = jnp.concatenate([jnp.stack([core, z, blk]).astype(jnp.int32), cols])
    return assemble(where, around, other)


def solution(mesh):
    placed = (P("blk", "branch"), P("blk"), P("branch"))
    return jax.shard_map(
        on_device, mesh=mesh, in_specs=placed, out_specs=P("blk", None), check_vma=False
    )
```

```python
import jax
import jax.numpy as jnp
from jax import lax
from jax.experimental import pallas as pl
from jax.experimental.pallas import tpu as pltpu
from jax.sharding import PartitionSpec as P

F32 = jnp.float32
BF16 = jnp.bfloat16
ROWS = 256
KS = 512
BLOCKS = 8
GROUP = 8
PAIRS = GROUP // 2
GROUPS = ROWS // GROUP


def block_at(y, x):
    return (y % 2) * 4 + x % 4


def partner_tables():
    first, second, third, fourth = [], [], [], []
    for b in range(BLOCKS):
        y, x = b // 4, b % 4
        first.append(block_at(y, x + 1))
        second.append(block_at(y + 1, x + 3))
        cycle = {(0, 0): (0, 2), (0, 1): (1, 2), (1, 1): (1, 0), (1, 0): (0, 0)}
        ny, nx = cycle[(y, x // 2)]
        third.append(block_at(ny, nx + x % 2))
        fourth.append(block_at(y + 1, x + 2))
    return [first, second, third, fourth]


PARTNERS = partner_tables()
OWNERS = [[table.index(b) for b in range(BLOCKS)] for table in PARTNERS]


def params():
    return pltpu.CompilerParams(vmem_limit_bytes=56 << 20)


def in_vmem(n):
    return [pl.BlockSpec(memory_space=pltpu.VMEM)] * n


def branch_sums(ref, lane):
    def add(k8, total):
        at = pl.ds(pl.multiple_of(k8 * 8, 8), 8)
        return total + ref[at, lane : lane + 128]

    total = lax.fori_loop(0, KS // 8, add, jnp.zeros((8, 128), F32), unroll=8)
    return jnp.sum(total, axis=0, keepdims=True)


def weigh_kernel(counts_ref, totals_ref, lengths_ref, wt_ref, split_ref, row_ref, col_ref):
    scaled = lengths_ref[...].astype(F32) * 0.001
    wt = (scaled * counts_ref[...].astype(F32)).T / totals_ref[...].astype(F32)
    wt_ref[...] = wt
    for n in range(8):
        x = wt[:, n * 32 : (n + 1) * 32]
        high = x.astype(BF16)
        rest = x - high.astype(F32)
        middle = rest.astype(BF16)
        low = (rest - middle.astype(F32)).astype(BF16)
        split_ref[n] = jnp.concatenate([high, middle, low, jnp.zeros_like(low)], axis=1)
    for h in range(2):
        sums = branch_sums(wt_ref, h * 128)
        row_ref[:, h * 128 : (h + 1) * 128] = jnp.broadcast_to(sums, (8, 128))
        col_ref[h * 128 : (h + 1) * 128, :] = jnp.broadcast_to(sums, (128, 128)).T


def weigh(counts, totals, lengths):
    return pl.pallas_call(
        weigh_kernel,
        out_shape=(
            jax.ShapeDtypeStruct((KS, ROWS), F32),
            jax.ShapeDtypeStruct((8, KS, 128), BF16),
            jax.ShapeDtypeStruct((8, ROWS), F32),
            jax.ShapeDtypeStruct((ROWS, 128), F32),
        ),
        compiler_params=params(),
        name="weigh",
    )(counts, totals.reshape(1, ROWS), lengths.reshape(1, KS))


def spread_call(name, n_blocks, columns, mass_lanes, width):
    def kernel(at_ref, split_ref, col_ref, *refs):
        blocks = refs[:n_blocks]
        out_ref, mass_ref, pick_ref, even_ref, odd_ref = refs[n_blocks:]
        core, y = at_ref[0], at_ref[1]

        part = lax.broadcasted_iota(jnp.int32, (128, 256), 0)
        lane = lax.broadcasted_iota(jnp.int32, (128, 256), 1)
        want = jnp.where(part < 96, part % 32 - lane // 128, -1)
        for p in range(16):
            pick_ref[p] = jnp.where(want == 2 * p, 1.0, 0.0).astype(BF16)

        sums = [branch_sums(blocks[n], lane) for n, lane in mass_lanes]
        block = jnp.concatenate(sums + [jnp.zeros((8 - len(sums), 128), F32)], axis=0)
        mass_ref[...] = block

        def mass_row(n, lane):
            if isinstance(lane, int):
                return sums[mass_lanes.index((n, lane))]
            first = sums[mass_lanes.index((n, 0))]
            return jnp.where(lane == 0, first, sums[mass_lanes.index((n, 128))])

        def broadcast_pair(into, g, q):
            pair = g * PAIRS + q
            into[q] = jnp.dot(
                split_ref[pair // 16], pick_ref[pair % 16], preferred_element_type=F32
            )

        def one_group(g, half, now, later):
            cols = columns(half, y)
            n_cols = len(cols)
            following = jnp.minimum(g + 1, GROUPS - 1)
            for q in range(PAIRS):
                broadcast_pair(later, following, q)
            acc = [jnp.zeros((8, 128), F32)] * (GROUP * n_cols)
            for k8 in range(KS // 8):
                at = slice(k8 * 8, k8 * 8 + 8)
                spans = [
                    blocks[n][at, lane : lane + 128]
                    if isinstance(lane, int)
                    else blocks[n][at, pl.ds(pl.multiple_of(lane, 128), 128)]
                    for n, lane in cols
                ]
                for r in range(GROUP):
                    own = now[r // 2, at, 128 * (r % 2) : 128 * (r % 2) + 128]
                    for j in range(n_cols):
                        acc[r * n_cols + j] += jnp.minimum(own, spans[j])
            side = jnp.where(half == core, 0, 1)
            own_mass = col_ref[pl.ds(pl.multiple_of(g * GROUP, 8), 8), :]
            row = pl.multiple_of((g - half * (GROUPS // 2)) * GROUP, 8)
            for j, (n, lane) in enumerate(cols):
                least = jnp.concatenate(
                    [jnp.sum(acc[r * n_cols + j], axis=0, keepdims=True) for r in range(GROUP)],
                    axis=0,
                )
                out_ref[side, pl.ds(row, 8), 128 * j : 128 * j + 128] = (
                    own_mass + mass_row(n, lane) - 2.0 * least
                )

        for q in range(PAIRS):
            broadcast_pair(even_ref, 0, q)

        for half in range(2):

            def two_groups(t, carry, half=half):
                g = half * (GROUPS // 2) + 2 * t
                one_group(g, half, even_ref, odd_ref)
                one_group(g + 1, half, odd_ref, even_ref)
                return carry

            lax.fori_loop(0, GROUPS // 4, two_groups, 0)

    steps = sum(len(columns(h, 0)) for h in range(2)) * 128 * 128 * KS

    def call(at, split, col, *blocks):
        return pl.pallas_call(
            kernel,
            out_shape=(
                jax.ShapeDtypeStruct((2, 128, width), F32),
                jax.ShapeDtypeStruct((8, 128), F32),
            ),
            in_specs=[pl.BlockSpec(memory_space=pltpu.SMEM)] + in_vmem(2 + n_blocks),
            out_specs=tuple(in_vmem(2)),
            scratch_shapes=[
                pltpu.VMEM((16, 128, 256), BF16),
                pltpu.VMEM((PAIRS, KS, 256), F32),
                pltpu.VMEM((PAIRS, KS, 256), F32),
            ],
            compiler_params=params(),
            cost_estimate=pl.CostEstimate(
                flops=steps * 250, bytes_accessed=4 << 20, transcendentals=0
            ),
            name=name,
        )(at, split, col, *blocks)

    return call


def diagonal_columns(half, y):
    return [(0, 128), (0, 0)][: 2 - half]


def first_columns(half, y):
    return [(0, 0), (0, 128), (1, 0), (1, 128)]


def second_columns(half, y):
    return [(0, 0), (0, 128), (1, (half ^ y) * 128)]


def assemble_kernel(at_ref, own1, other1, own2, other2, out_ref, all_ref):
    core, y = at_ref[0], at_ref[1]
    n1 = own1.shape[2]
    for c, ref1, ref2 in ((core, own1, own2), (1 - core, other1, other2)):
        to = pl.ds(pl.multiple_of(c * 128, 128), 128)
        all_ref[to, 0:n1] = ref1[...].reshape(128, n1)
        all_ref[to, n1:] = ref2[...].reshape(128, all_ref.shape[1] - n1)

    def columns(slot, half=None):
        first = at_ref[2 + slot] * ROWS
        if half is None:
            return pl.ds(pl.multiple_of(first, ROWS), ROWS)
        return pl.ds(pl.multiple_of(first + half * 128, 128), 128)

    upper = all_ref[0:128, 0:128]
    out_ref[0:128, columns(0, 0)] = all_ref[0:128, 128:256]
    out_ref[0:128, columns(0, 1)] = upper
    out_ref[128:256, columns(0, 0)] = upper.T
    out_ref[128:256, columns(0, 1)] = all_ref[128:256, 0:128]
    for slot, lane in ((1, 256), (2, 512), (3, n1)):
        out_ref[:, columns(slot)] = all_ref[:, lane : lane + ROWS]
    for slot, lane in ((5, 768), (6, 1024), (7, n1 + 384)):
        out_ref[:, columns(slot)] = all_ref[:, lane : lane + ROWS].T
    for half in range(2):
        rows = slice(half * 128, half * 128 + 128)
        out_ref[rows, columns(4, half ^ y)] = all_ref[rows, n1 + 256 : n1 + 384]
        to = pl.ds(pl.multiple_of((half ^ (1 - y)) * 128, 128), 128)
        out_ref[to, columns(4, half)] = all_ref[rows, n1 + 640 : n1 + 768].T


def assemble(at, own1, other1, own2, other2):
    return pl.pallas_call(
        assemble_kernel,
        out_shape=jax.ShapeDtypeStruct((ROWS, BLOCKS * ROWS), F32),
        in_specs=[pl.BlockSpec(memory_space=pltpu.SMEM)] + in_vmem(4),
        out_specs=in_vmem(1)[0],
        scratch_shapes=[pltpu.VMEM((ROWS, own1.shape[2] + own2.shape[2]), F32)],
        compiler_params=params(),
        name="assemble",
    )(at, own1, other1, own2, other2)


def on_device(counts, totals, lengths):
    blk = lax.axis_index("blk")
    branch = lax.axis_index("branch")
    core, place = branch % 2, branch // 2
    y_hi = blk // 4
    tables = jnp.array([list(range(BLOCKS))] + PARTNERS + OWNERS[:3], jnp.int32)
    slots = lax.dynamic_index_in_dim(tables, blk, 1, False)
    at = jnp.concatenate([jnp.stack([core, y_hi]).astype(jnp.int32), slots])

    def from_partner(v, n):
        return lax.ppermute(v, "blk", [(PARTNERS[n][b], b) for b in range(BLOCKS)])

    def to_partner(v, n):
        return lax.ppermute(v, "blk", [(b, PARTNERS[n][b]) for b in range(BLOCKS)])

    def other_core(v):
        return lax.ppermute(v, "branch", [(i, i ^ 1) for i in range(32)])

    chips = [[2 * p + c for p in range(16)] for c in range(2)]

    def over_chips(v):
        return lax.all_to_all(v, "branch", 0, 0, axis_index_groups=chips)

    wt, split, mass_row, mass_col = weigh(counts, totals, lengths)
    got = [from_partner(wt, n) for n in range(4)]

    diagonal = spread_call("diagonal", 1, diagonal_columns, [(0, 0), (0, 128)], 256)
    first = spread_call(
        "first", 2, first_columns, [(0, 0), (0, 128), (1, 0), (1, 128)], 512
    )
    second = spread_call(
        "second", 2, second_columns, [(0, 0), (0, 128), (1, 0), (1, 128)], 384
    )

    def on_chip(parts):
        out, mass = parts
        return out[0] + other_core(out[1]), mass + other_core(mass)

    def scatter(tiles, masses):
        tiles = jnp.concatenate(tiles, axis=1).reshape(16, 8, -1)
        masses = jnp.broadcast_to(masses[None], (16, 8, 128))
        shard = jnp.sum(over_chips(jnp.concatenate([tiles, masses], axis=2)), axis=0)
        return shard[:, :-128], shard[:, -128:]

    def gather(pieces):
        mine = jnp.concatenate(pieces, axis=1)
        whole = over_chips(jnp.broadcast_to(mine[None], (16, *mine.shape)))
        return whole, other_core(whole)

    tile0, sums0 = on_chip(diagonal(at, split, mass_col, wt))
    tile1, sums1 = on_chip(first(at, split, mass_col, got[0], got[1]))
    tile2, sums2 = on_chip(second(at, split, mass_col, got[2], got[3]))

    sums = jnp.concatenate([sums0[0:2], sums1[0:4], sums0[6:8]])
    shard, sums = scatter([tile0, tile1], sums)
    own_mass = lax.dynamic_slice_in_dim(
        sums[0:2].reshape(ROWS), core * 128 + place * 8, 8
    )[:, None]
    parts = jnp.concatenate([sums[1], sums[0], sums[2:6].reshape(512)])
    dist1 = shard / (own_mass + parts[None, :])
    swapped1 = [to_partner(dist1[:, 256 * (n + 1) : 256 * (n + 2)], n) for n in range(2)]
    own1, other1 = gather([dist1, *swapped1])

    shard, sums = scatter([tile2], sums2)
    last = jnp.where((core ^ y_hi) == 0, sums[2], sums[3])
    parts = jnp.concatenate([sums[0], sums[1], last])
    dist2 = shard / (own_mass + parts[None, :])
    swapped2 = [to_partner(dist2[:, 0:256], 2), to_partner(dist2[:, 256:384], 3)]
    own2, other2 = gather([dist2, *swapped2])

    return assemble(at, own1, other1, own2, other2)


def solution(mesh):
    placed = (P("blk", "branch"), P("blk"), P("branch"))
    return jax.shard_map(
        on_device, mesh=mesh, in_specs=placed, out_specs=P("blk", None), check_vma=False
    )
```

```python
import jax
import jax.numpy as jnp
from jax import lax
from jax.experimental import pallas as pl
from jax.experimental.pallas import tpu as pltpu
from jax.sharding import PartitionSpec as P

F32 = jnp.float32
BF16 = jnp.bfloat16
ROWS = 256
KS = 512
BLOCKS = 8
GROUP = 8
PAIRS = GROUP // 2
GROUPS = ROWS // GROUP


def block_at(y, x):
    return (y % 2) * 4 + x % 4


def partner_tables():
    first, second, third, fourth = [], [], [], []
    for b in range(BLOCKS):
        y, x = b // 4, b % 4
        first.append(block_at(y, x + 1))
        second.append(block_at(y + 1, x + 3))
        cycle = {(0, 0): (0, 2), (0, 1): (1, 2), (1, 1): (1, 0), (1, 0): (0, 0)}
        ny, nx = cycle[(y, x // 2)]
        third.append(block_at(ny, nx + x % 2))
        fourth.append(block_at(y + 1, x + 2))
    return [first, second, third, fourth]


PARTNERS = partner_tables()
OWNERS = [[table.index(b) for b in range(BLOCKS)] for table in PARTNERS]


def params():
    return pltpu.CompilerParams(vmem_limit_bytes=56 << 20)


def in_vmem(n):
    return [pl.BlockSpec(memory_space=pltpu.VMEM)] * n


def branch_sums(ref, lane):
    def add(k8, total):
        at = pl.ds(pl.multiple_of(k8 * 8, 8), 8)
        return total + ref[at, lane : lane + 128]

    total = lax.fori_loop(0, KS // 8, add, jnp.zeros((8, 128), F32), unroll=8)
    return jnp.sum(total, axis=0, keepdims=True)


def weigh_kernel(counts_ref, totals_ref, lengths_ref, wt_ref, split_ref, row_ref, col_ref):
    scaled = lengths_ref[...].astype(F32) * 0.001
    wt = (scaled * counts_ref[...].astype(F32)).T / totals_ref[...].astype(F32)
    wt_ref[...] = wt
    for n in range(8):
        x = wt[:, n * 32 : (n + 1) * 32]
        high = x.astype(BF16)
        rest = x - high.astype(F32)
        middle = rest.astype(BF16)
        low = (rest - middle.astype(F32)).astype(BF16)
        split_ref[n] = jnp.concatenate([high, middle, low, jnp.zeros_like(low)], axis=1)
    for h in range(2):
        sums = branch_sums(wt_ref, h * 128)
        row_ref[:, h * 128 : (h + 1) * 128] = jnp.broadcast_to(sums, (8, 128))
        col_ref[h * 128 : (h + 1) * 128, :] = jnp.broadcast_to(sums, (128, 128)).T


def weigh(counts, totals, lengths):
    return pl.pallas_call(
        weigh_kernel,
        out_shape=(
            jax.ShapeDtypeStruct((KS, ROWS), F32),
            jax.ShapeDtypeStruct((8, KS, 128), BF16),
            jax.ShapeDtypeStruct((8, ROWS), F32),
            jax.ShapeDtypeStruct((ROWS, 128), F32),
        ),
        compiler_params=params(),
        name="weigh",
    )(counts, totals.reshape(1, ROWS), lengths.reshape(1, KS))


def spread_call(name, n_blocks, columns, sides, width, group=8, mass_row=0):
    pairs = group // 2
    groups = ROWS // 2 // group

    def kernel(split_ref, col_ref, *refs):
        blocks = refs[:n_blocks]
        outs = refs[n_blocks : n_blocks + len(sides)]
        pick_ref, even_ref, odd_ref = refs[n_blocks + len(sides) :]
        core = lax.axis_index("branch") % 2
        y = lax.axis_index("blk") // 4

        part = lax.broadcasted_iota(jnp.int32, (128, 256), 0)
        lane = lax.broadcasted_iota(jnp.int32, (128, 256), 1)
        want = jnp.where(part < 96, part % 32 - lane // 128, -1)
        for p in range(16):
            pick_ref[p] = jnp.where(want == 2 * p, 1.0, 0.0).astype(BF16)

        def span(n, lane, at):
            if isinstance(lane, int):
                return blocks[n][at, lane : lane + 128]
            return blocks[n][at, pl.ds(pl.multiple_of(lane, 128), 128)]

        def broadcast_pair(into, g, q, at=slice(0, KS)):
            pair = g * pairs + q
            into[q, at] = jnp.dot(
                split_ref[pair // 16, at], pick_ref[pair % 16], preferred_element_type=F32
            )

        def one_group(g, base, out_ref, cols, sums, now, later):
            n_cols = len(cols)
            following = jnp.minimum(base + g + 1, ROWS // group - 1)
            steps = []
            if group == 8:
                for q in range(pairs):
                    broadcast_pair(later, following, q)
            else:
                steps = [(q, slice(k, k + 128)) for k in range(0, KS, 128) for q in range(pairs)]
            acc = [jnp.zeros((8, 128), F32)] * (group * n_cols)
            for k8 in range(KS // 8):
                if steps and k8 % 2 == 0:
                    q, at = steps[k8 // 2]
                    broadcast_pair(later, following, q, at)
                at = slice(k8 * 8, k8 * 8 + 8)
                spans = [span(n, lane, at) for n, lane in cols]
                for r in range(group):
                    own = now[r // 2, at, 128 * (r % 2) : 128 * (r % 2) + 128]
                    for j in range(n_cols):
                        acc[r * n_cols + j] += jnp.minimum(own, spans[j])
            for r0 in range(0, group, 8):
                row = pl.multiple_of(g * group + r0, 8)
                own_mass = col_ref[pl.ds(pl.multiple_of(base * group + row, 8), 8), :]
                for j in range(n_cols):
                    least = jnp.concatenate(
                        [
                            jnp.sum(acc[(r0 + r) * n_cols + j], axis=0, keepdims=True)
                            for r in range(8)
                        ],
                        axis=0,
                    )
                    out_ref[pl.ds(row, 8), 128 * j : 128 * j + 128] = (
                        own_mass + sums[j] - 2.0 * least
                    )

        def one_side(out_ref, half, cols):
            base = half * groups
            sums = []
            for n, lane in cols:
                total = jnp.zeros((8, 128), F32)
                for k8 in range(KS // 8):
                    total = total + span(n, lane, slice(k8 * 8, k8 * 8 + 8))
                sums.append(jnp.sum(total, axis=0, keepdims=True))
            zeros = jnp.zeros((1, 128), F32)
            below = [zeros] * mass_row + sums
            below = below + [zeros] * (8 - len(below))
            out_ref[128:136, 0:128] = jnp.concatenate(below, axis=0)
            for q in range(pairs):
                broadcast_pair(even_ref, base, q)

            def two_groups(t, carry):
                one_group(2 * t, base, out_ref, cols, sums, even_ref, odd_ref)
                one_group(2 * t + 1, base, out_ref, cols, sums, odd_ref, even_ref)
                return carry

            lax.fori_loop(0, groups // 2, two_groups, 0)

        for side, out_ref in zip(sides, outs, strict=True):
            half = core if side == 0 else 1 - core
            if isinstance(columns, tuple):
                for value, cols in enumerate(columns):
                    pl.when(half == value)(
                        lambda out_ref=out_ref, half=half, cols=cols: one_side(out_ref, half, cols)
                    )
            else:
                one_side(out_ref, half, columns(half, y))

    steps = width * 128 * KS * len(sides)

    def call(split, col, *blocks):
        return pl.pallas_call(
            kernel,
            out_shape=tuple(jax.ShapeDtypeStruct((136, width), F32) for _ in sides),
            in_specs=in_vmem(2 + n_blocks),
            out_specs=tuple(in_vmem(len(sides))),
            scratch_shapes=[
                pltpu.VMEM((16, 128, 256), BF16),
                pltpu.VMEM((pairs, KS, 256), F32),
                pltpu.VMEM((pairs, KS, 256), F32),
            ],
            compiler_params=params(),
            cost_estimate=pl.CostEstimate(
                flops=steps * 250, bytes_accessed=4 << 20, transcendentals=0
            ),
            name=name,
        )(split, col, *blocks)

    return call


DIAGONAL = ([(0, 128), (0, 0)], [(0, 128)])


def first_columns(half, y):
    return [(0, 0), (0, 128), (1, 0), (1, 128)]


def second_columns(half, y):
    return [(0, 0), (0, 128), (1, (half ^ y) * 128)]


def block_partner(b, slot):
    y, x = b // 4, b % 4
    if slot == 0:
        return b
    if slot == 1:
        return y * 4 + (x + 1) % 4
    if slot == 2:
        return (1 - y) * 4 + (x + 3) % 4
    if slot == 4:
        return (1 - y) * 4 + (x + 2) % 4
    if slot == 5:
        return y * 4 + (x + 3) % 4
    if slot == 6:
        return (1 - y) * 4 + (x + 1) % 4
    far = x // 2
    keep_y = (far == y) if slot == 3 else (far != y)
    return jnp.where(keep_y, y * 4 + (x + 2) % 4, (1 - y) * 4 + x)


def assemble_kernel(own1, other1, own2, other2, out_ref, all_ref):
    core = lax.axis_index("branch") % 2
    b = lax.axis_index("blk")
    y = b // 4
    n1 = own1.shape[2]
    for c, ref1, ref2 in ((core, own1, own2), (1 - core, other1, other2)):
        to = pl.ds(pl.multiple_of(c * 128, 128), 128)
        all_ref[to, 0:n1] = ref1[...].reshape(128, n1)
        all_ref[to, n1:] = ref2[...].reshape(128, all_ref.shape[1] - n1)

    def columns(slot, half=None):
        first = block_partner(b, slot) * ROWS
        if half is None:
            return pl.ds(pl.multiple_of(first, ROWS), ROWS)
        return pl.ds(pl.multiple_of(first + half * 128, 128), 128)

    upper = all_ref[0:128, 0:128]
    out_ref[0:128, columns(0, 0)] = all_ref[0:128, 128:256]
    out_ref[0:128, columns(0, 1)] = upper
    out_ref[128:256, columns(0, 0)] = upper.T
    out_ref[128:256, columns(0, 1)] = all_ref[128:256, 0:128]
    for slot, lane in ((1, 256), (2, 512), (3, n1)):
        out_ref[:, columns(slot)] = all_ref[:, lane : lane + ROWS]
    for slot, lane in ((5, 768), (6, 1024), (7, n1 + 384)):
        out_ref[:, columns(slot)] = all_ref[:, lane : lane + ROWS].T
    for half in range(2):
        rows = slice(half * 128, half * 128 + 128)
        out_ref[rows, columns(4, half ^ y)] = all_ref[rows, n1 + 256 : n1 + 384]
        to = pl.ds(pl.multiple_of((half ^ (1 - y)) * 128, 128), 128)
        out_ref[to, columns(4, half)] = all_ref[rows, n1 + 640 : n1 + 768].T


def assemble(own1, other1, own2, other2):
    return pl.pallas_call(
        assemble_kernel,
        out_shape=jax.ShapeDtypeStruct((ROWS, BLOCKS * ROWS), F32),
        in_specs=in_vmem(4),
        out_specs=in_vmem(1)[0],
        scratch_shapes=[pltpu.VMEM((ROWS, own1.shape[2] + own2.shape[2]), F32)],
        compiler_params=params(),
        name="assemble",
    )(own1, other1, own2, other2)


def on_device(counts, totals, lengths):
    branch = lax.axis_index("branch")
    place = branch // 2

    def from_partner(v, n):
        return lax.ppermute(v, "blk", [(PARTNERS[n][b], b) for b in range(BLOCKS)])

    def to_partner(v, n):
        return lax.ppermute(v, "blk", [(b, PARTNERS[n][b]) for b in range(BLOCKS)])

    def other_core(v):
        return lax.ppermute(v, "branch", [(i, i ^ 1) for i in range(32)])

    chips = [[2 * p + c for p in range(16)] for c in range(2)]

    def over_chips(v):
        return lax.all_to_all(v, "branch", 0, 0, axis_index_groups=chips)

    def scatter(kept, received):
        tiles = jnp.concatenate(
            [(k[:128] + r[:128]).reshape(16, 8, -1) for k, r in zip(kept, received, strict=True)],
            axis=2,
        )
        masses = sum(k[128:, :128] + r[128:, :128] for k, r in zip(kept, received, strict=True))
        masses = jnp.broadcast_to(masses[None], (16, 8, 128))
        shard = jnp.sum(over_chips(jnp.concatenate([tiles, masses], axis=2)), axis=0)
        return shard[:, :-128], shard[:, -128:]

    def gather(pieces):
        mine = jnp.concatenate(pieces, axis=1)
        whole = over_chips(jnp.broadcast_to(mine[None], (16, *mine.shape)))
        return whole, other_core(whole)

    wt, split, mass_row, mass_col = weigh(counts, totals, lengths)
    got = [from_partner(wt, n) for n in range(2)]
    diagonal = spread_call("diagonal", 1, DIAGONAL, (1, 0), 256, group=16, mass_row=4)
    first = spread_call("first", 2, first_columns, (1, 0), 512)
    second = [spread_call(f"second{s}", 2, second_columns, (s,), 384) for s in range(2)]

    send0, keep0 = diagonal(split, mass_col, wt)
    later, keep0 = lax.optimization_barrier((wt, keep0))
    got += [from_partner(later, n) for n in (2, 3)]
    send1, keep1 = first(split, mass_col, got[0], got[1])
    shard, sums = scatter([keep0, keep1], [other_core(send0), other_core(send1)])
    (send2,) = second[1](split, mass_col, got[2], got[3])
    (keep2,) = second[0](split, mass_col, got[2], got[3])

    own_lower = sums[5]
    own_half = jnp.where(branch % 2 == 0, own_lower, sums[4])
    own_mass = lax.dynamic_slice_in_dim(own_half, place * 8, 8)[:, None]
    parts = jnp.concatenate([sums[4:5], sums[5:6], sums[0:4]]).reshape(768)
    dist1 = shard / (own_mass + parts[None, :])
    swapped1 = [to_partner(dist1[:, 256 * (n + 1) : 256 * (n + 2)], n) for n in range(2)]
    own1, other1 = gather([dist1, *swapped1])

    shard, sums = scatter([keep2], [other_core(send2)])
    dist2 = shard / (own_mass + sums[0:3].reshape(384)[None, :])
    swapped2 = [to_partner(dist2[:, 0:256], 2), to_partner(dist2[:, 256:384], 3)]
    own2, other2 = gather([dist2, *swapped2])

    return assemble(own1, other1, own2, other2)


def solution(mesh):
    placed = (P("blk", "branch"), P("blk"), P("branch"))
    return jax.shard_map(
        on_device, mesh=mesh, in_specs=placed, out_specs=P("blk", None), check_vma=False
    )
```

```python
import jax
import jax.numpy as jnp
from jax import lax
from jax.experimental import pallas as pl
from jax.experimental.pallas import tpu as pltpu
from jax.sharding import PartitionSpec as P

F32 = jnp.float32
BF16 = jnp.bfloat16
ROWS = 256
KS = 512
BLOCKS = 8
GROUP = 8
PAIRS = GROUP // 2
GROUPS = ROWS // GROUP


def block_at(y, x):
    return (y % 2) * 4 + x % 4


def partner_tables():
    first, second, third, fourth = [], [], [], []
    for b in range(BLOCKS):
        y, x = b // 4, b % 4
        first.append(block_at(y, x + 1))
        second.append(block_at(y + 1, x + 3))
        cycle = {(0, 0): (0, 2), (0, 1): (1, 2), (1, 1): (1, 0), (1, 0): (0, 0)}
        ny, nx = cycle[(y, x // 2)]
        third.append(block_at(ny, nx + x % 2))
        fourth.append(block_at(y + 1, x + 2))
    return [first, second, third, fourth]


PARTNERS = partner_tables()
OWNERS = [[table.index(b) for b in range(BLOCKS)] for table in PARTNERS]


def params():
    return pltpu.CompilerParams(vmem_limit_bytes=56 << 20)


def in_vmem(n):
    return [pl.BlockSpec(memory_space=pltpu.VMEM)] * n


def branch_sums(ref, lane):
    def add(k8, total):
        at = pl.ds(pl.multiple_of(k8 * 8, 8), 8)
        return total + ref[at, lane : lane + 128]

    total = lax.fori_loop(0, KS // 8, add, jnp.zeros((8, 128), F32), unroll=8)
    return jnp.sum(total, axis=0, keepdims=True)


def weigh_kernel(counts_ref, totals_ref, lengths_ref, wt_ref, split_ref, row_ref, col_ref):
    scaled = lengths_ref[...].astype(F32) * 0.001
    wt = (scaled * counts_ref[...].astype(F32)).T / totals_ref[...].astype(F32)
    wt_ref[...] = wt
    for n in range(8):
        x = wt[:, n * 32 : (n + 1) * 32]
        high = x.astype(BF16)
        rest = x - high.astype(F32)
        middle = rest.astype(BF16)
        low = (rest - middle.astype(F32)).astype(BF16)
        split_ref[n] = jnp.concatenate([high, middle, low, jnp.zeros_like(low)], axis=1)
    for h in range(2):
        sums = branch_sums(wt_ref, h * 128)
        row_ref[:, h * 128 : (h + 1) * 128] = jnp.broadcast_to(sums, (8, 128))
        col_ref[h * 128 : (h + 1) * 128, :] = jnp.broadcast_to(sums, (128, 128)).T


def weigh(counts, totals, lengths):
    return pl.pallas_call(
        weigh_kernel,
        out_shape=(
            jax.ShapeDtypeStruct((KS, ROWS), F32),
            jax.ShapeDtypeStruct((8, KS, 128), BF16),
            jax.ShapeDtypeStruct((8, ROWS), F32),
            jax.ShapeDtypeStruct((ROWS, 128), F32),
        ),
        compiler_params=params(),
        name="weigh",
    )(counts, totals.reshape(1, ROWS), lengths.reshape(1, KS))


def spread_call(name, n_blocks, columns, width, group, mass_row):
    pairs = group // 2
    groups = ROWS // group

    def kernel(split_ref, col_ref, *refs):
        sources = refs[:n_blocks]
        out_ref = refs[n_blocks]
        block_ref, pick_ref, even_ref, odd_ref, sems = refs[n_blocks + 1 :]
        y = lax.axis_index("blk") // 4

        loads = [
            pltpu.make_async_copy(src, block_ref.at[n], sems.at[n])
            for n, src in enumerate(sources)
        ]
        for load in loads:
            load.start()

        part = lax.broadcasted_iota(jnp.int32, (128, 256), 0)
        lane = lax.broadcasted_iota(jnp.int32, (128, 256), 1)
        want = jnp.where(part < 96, part % 32 - lane // 128, -1)
        for p in range(16):
            pick_ref[p] = jnp.where(want == 2 * p, 1.0, 0.0).astype(BF16)

        def broadcast_pair(into, g, q, at=slice(0, KS)):
            pair = g * pairs + q
            into[q, at] = jnp.dot(
                split_ref[pair // 16, at], pick_ref[pair % 16], preferred_element_type=F32
            )

        for q in range(pairs):
            broadcast_pair(even_ref, 0, q)
        for load in loads:
            load.wait()

        def span(n, lane, at):
            if isinstance(lane, int):
                return block_ref[n, at, lane : lane + 128]
            return block_ref[n, at, pl.ds(pl.multiple_of(lane, 128), 128)]

        for half in range(2):
            below = [jnp.zeros((1, 128), F32)] * mass_row
            for n, lane in columns(half, y):
                total = jnp.zeros((8, 128), F32)
                for k8 in range(KS // 8):
                    total = total + span(n, lane, slice(k8 * 8, k8 * 8 + 8))
                below.append(jnp.sum(total, axis=0, keepdims=True))
            below += [jnp.zeros((1, 128), F32)] * (8 - len(below))
            out_ref[half, 128:136, 0:128] = jnp.concatenate(below, axis=0)

        def one_group(g, now, later):
            half = g // (groups // 2)
            cols = columns(half, y)
            n_cols = len(cols)
            following = jnp.minimum(g + 1, groups - 1)
            steps = []
            if group == 8:
                for q in range(pairs):
                    broadcast_pair(later, following, q)
            else:
                steps = [(q, slice(k, k + 128)) for k in range(0, KS, 128) for q in range(pairs)]
            acc = [jnp.zeros((8, 128), F32)] * (group * n_cols)
            for k8 in range(KS // 8):
                if steps and k8 % 2 == 0:
                    q, at = steps[k8 // 2]
                    broadcast_pair(later, following, q, at)
                at = slice(k8 * 8, k8 * 8 + 8)
                spans = [span(n, lane, at) for n, lane in cols]
                for r in range(group):
                    own = now[r // 2, at, 128 * (r % 2) : 128 * (r % 2) + 128]
                    for j in range(n_cols):
                        acc[r * n_cols + j] += jnp.minimum(own, spans[j])
            for r0 in range(0, group, 8):
                first = pl.multiple_of(g * group + r0, 8)
                row = pl.multiple_of(first - half * 128, 8)
                own_mass = col_ref[pl.ds(first, 8), :]
                for j in range(n_cols):
                    mass = out_ref[half, 128 + mass_row + j : 129 + mass_row + j, 0:128]
                    least = jnp.concatenate(
                        [
                            jnp.sum(acc[(r0 + r) * n_cols + j], axis=0, keepdims=True)
                            for r in range(8)
                        ],
                        axis=0,
                    )
                    out_ref[half, pl.ds(row, 8), 128 * j : 128 * j + 128] = (
                        own_mass + mass - 2.0 * least
                    )

        def two_groups(t, carry):
            one_group(2 * t, even_ref, odd_ref)
            one_group(2 * t + 1, odd_ref, even_ref)
            return carry

        lax.fori_loop(0, groups // 2, two_groups, 0)

    def call(split, col, *blocks):
        return pl.pallas_call(
            kernel,
            out_shape=jax.ShapeDtypeStruct((2, 136, width), F32),
            in_specs=in_vmem(2) + [pl.BlockSpec(memory_space=pl.ANY)] * n_blocks,
            out_specs=in_vmem(1)[0],
            scratch_shapes=[
                pltpu.VMEM((n_blocks, KS, ROWS), F32),
                pltpu.VMEM((16, 128, 256), BF16),
                pltpu.VMEM((pairs, KS, 256), F32),
                pltpu.VMEM((pairs, KS, 256), F32),
                pltpu.SemaphoreType.DMA((n_blocks,)),
            ],
            compiler_params=params(),
            cost_estimate=pl.CostEstimate(
                flops=width * ROWS * KS * 250, bytes_accessed=4 << 20, transcendentals=0
            ),
            name=name,
        )(split, col, *blocks)

    return call


def diagonal_columns(half, y):
    return [(0, 128), (0, 0)]


def first_columns(half, y):
    return [(0, 0), (0, 128), (1, 0), (1, 128)]


def second_columns(half, y):
    return [(0, 0), (0, 128), (1, (half ^ y) * 128)]


def block_partner(b, slot):
    y, x = b // 4, b % 4
    if slot == 0:
        return b
    if slot == 1:
        return y * 4 + (x + 1) % 4
    if slot == 2:
        return (1 - y) * 4 + (x + 3) % 4
    if slot == 4:
        return (1 - y) * 4 + (x + 2) % 4
    if slot == 5:
        return y * 4 + (x + 3) % 4
    if slot == 6:
        return (1 - y) * 4 + (x + 1) % 4
    far = x // 2
    keep_y = (far == y) if slot == 3 else (far != y)
    return jnp.where(keep_y, y * 4 + (x + 2) % 4, (1 - y) * 4 + x)


DIRECT = 1152
SWAPPED = 896


def assemble_kernel(own1, other1, own2, other2, out_ref, all_ref, turned_ref, sems, out_sems):
    core = lax.axis_index("branch") % 2
    b = lax.axis_index("blk")
    y = b // 4
    loads = []
    for n, (ref, c, lane) in enumerate(
        ((own2, core, DIRECT), (other2, 1 - core, DIRECT), (own1, core, 0), (other1, 1 - core, 0))
    ):
        to = pl.ds(pl.multiple_of(c * 128, 128), 128)
        into = all_ref.at[to, lane : lane + ref.shape[1]]
        loads.append(pltpu.make_async_copy(ref, into, sems.at[n]))
    for load in loads:
        load.start()

    def columns(slot, half=None):
        first = block_partner(b, slot) * ROWS
        if half is None:
            return pl.ds(pl.multiple_of(first, ROWS), ROWS)
        return pl.ds(pl.multiple_of(first + half * 128, 128), 128)

    stores = []

    def store(src, rows, cols):
        copy = pltpu.make_async_copy(src, out_ref.at[rows, cols], out_sems.at[len(stores)])
        copy.start()
        stores.append(copy)

    every = slice(0, ROWS)
    for load in loads:
        load.wait()
    for slot, lane in ((1, 256), (2, 512), (3, 768)):
        store(all_ref.at[:, lane : lane + ROWS], every, columns(slot))
    for half in range(2):
        rows = slice(half * 128, half * 128 + 128)
        store(all_ref.at[rows, 1024:1152], rows, columns(4, half ^ y))
        store(all_ref.at[:, 128 - half * 128 : 256 - half * 128], every, columns(0, half))
    for n, slot in enumerate((5, 6, 7)):
        lane = DIRECT + n * ROWS
        turned_ref[n] = all_ref[:, lane : lane + ROWS].T
        store(turned_ref.at[n], every, columns(slot))
    for half in range(2):
        at = slice(half * 128, half * 128 + 128)
        turned_ref[3, 0:128, at] = all_ref[at, DIRECT + 768 : DIRECT + 896].T
        to = pl.ds(pl.multiple_of((half ^ (1 - y)) * 128, 128), 128)
        store(turned_ref.at[3, 0:128, at], to, columns(4, half))
    for copy in stores:
        copy.wait()


def assemble(*pieces):
    anywhere = pl.BlockSpec(memory_space=pl.ANY)
    return pl.pallas_call(
        assemble_kernel,
        out_shape=jax.ShapeDtypeStruct((ROWS, BLOCKS * ROWS), F32),
        in_specs=[anywhere] * 4,
        out_specs=anywhere,
        scratch_shapes=[
            pltpu.VMEM((ROWS, DIRECT + SWAPPED), F32),
            pltpu.VMEM((4, ROWS, ROWS), F32),
            pltpu.SemaphoreType.DMA((4,)),
            pltpu.SemaphoreType.DMA((12,)),
        ],
        compiler_params=params(),
        name="assemble",
    )(*[p.reshape(128, p.shape[2]) for p in pieces])


def on_device(counts, totals, lengths):
    branch = lax.axis_index("branch")
    place = branch // 2

    def from_partner(v, n):
        return lax.ppermute(v, "blk", [(PARTNERS[n][b], b) for b in range(BLOCKS)])

    def to_partner(v, n):
        return lax.ppermute(v, "blk", [(b, PARTNERS[n][b]) for b in range(BLOCKS)])

    def other_core(v):
        return lax.ppermute(v, "branch", [(i, i ^ 1) for i in range(32)])

    chips = [[2 * p + c for p in range(16)] for c in range(2)]

    def over_chips(v):
        return lax.all_to_all(v, "branch", 0, 0, axis_index_groups=chips)

    def gather(pieces):
        mine = jnp.concatenate(pieces, axis=1)
        whole = over_chips(jnp.broadcast_to(mine[None], (16, *mine.shape)))
        return whole, other_core(whole)

    wt, split, mass_row, mass_col = weigh(counts, totals, lengths)
    got = [from_partner(wt, n) for n in range(2)]
    diagonal = spread_call("diagonal", 1, diagonal_columns, 256, 16, 0)
    first = spread_call("first", 2, first_columns, 512, 8, 2)
    second = spread_call("second", 2, second_columns, 384, 8, 0)

    part0 = diagonal(split, mass_col, wt)
    later, part0 = lax.optimization_barrier((wt, part0))
    got += [from_partner(later, n) for n in (2, 3)]
    part1 = first(split, mass_col, got[0], got[1])
    part2 = second(split, mass_col, got[2], got[3])

    def on_chip(part):
        both = part + other_core(part)
        return lax.dynamic_index_in_dim(both, branch % 2, 0, False)

    parts = [on_chip(part) for part in (part0, part1, part2)]
    tiles = [p[:128].reshape(16, 8, -1) for p in parts]
    masses = [
        jnp.broadcast_to(m[None], (16, 8, 128))
        for m in (parts[0][128:, :128] + parts[1][128:, :128], parts[2][128:, :128])
    ]
    shard = jnp.sum(over_chips(jnp.concatenate(tiles + masses, axis=2)), axis=0)

    mass = shard[:, DIRECT : DIRECT + 128]
    own_half = jnp.where(branch % 2 == 0, mass[1], mass[0])
    own_mass = lax.dynamic_slice_in_dim(own_half, place * 8, 8)[:, None]
    parts = jnp.concatenate([mass[0:6], shard[0:3, DIRECT + 128 :]]).reshape(DIRECT)
    dist = shard[:, :DIRECT] / (own_mass + parts[None, :])
    swapped = [
        to_partner(dist[:, 256 * (n + 1) : min(256 * (n + 2), DIRECT)], n) for n in range(4)
    ]
    own1, other1 = gather([dist])
    own2, other2 = gather(swapped)
    return assemble(own1, other1, own2, other2)


def solution(mesh):
    placed = (P("blk", "branch"), P("blk"), P("branch"))
    return jax.shard_map(
        on_device, mesh=mesh, in_specs=placed, out_specs=P("blk", None), check_vma=False
    )
```

```python
import jax
import jax.numpy as jnp
from jax import lax
from jax.experimental import pallas as pl
from jax.experimental.pallas import tpu as pltpu
from jax.sharding import PartitionSpec as P

F32 = jnp.float32
BF16 = jnp.bfloat16
ROWS = 256
KS = 512
BLOCKS = 8
GROUP = 8
PAIRS = GROUP // 2
GROUPS = ROWS // GROUP


def block_at(y, x):
    return (y % 2) * 4 + x % 4


def partner_tables():
    first, second, third, fourth = [], [], [], []
    for b in range(BLOCKS):
        y, x = b // 4, b % 4
        first.append(block_at(y, x + 1))
        second.append(block_at(y + 1, x + 3))
        cycle = {(0, 0): (0, 2), (0, 1): (1, 2), (1, 1): (1, 0), (1, 0): (0, 0)}
        ny, nx = cycle[(y, x // 2)]
        third.append(block_at(ny, nx + x % 2))
        fourth.append(block_at(y + 1, x + 2))
    return [first, second, third, fourth]


PARTNERS = partner_tables()
OWNERS = [[table.index(b) for b in range(BLOCKS)] for table in PARTNERS]


def params():
    return pltpu.CompilerParams(vmem_limit_bytes=24 << 20)


def in_vmem(n):
    return [pl.BlockSpec(memory_space=pltpu.VMEM)] * n


def branch_sums(ref, lane):
    def add(k8, total):
        at = pl.ds(pl.multiple_of(k8 * 8, 8), 8)
        return total + ref[at, lane : lane + 128]

    total = lax.fori_loop(0, KS // 8, add, jnp.zeros((8, 128), F32), unroll=8)
    return jnp.sum(total, axis=0, keepdims=True)


def weigh_kernel(counts_ref, totals_ref, lengths_ref, wt_ref, split_ref, row_ref, col_ref):
    scaled = lengths_ref[...].astype(F32) * 0.001
    wt = (scaled * counts_ref[...].astype(F32)).T / totals_ref[...].astype(F32)
    wt_ref[...] = wt
    for n in range(8):
        x = wt[:, n * 32 : (n + 1) * 32]
        high = x.astype(BF16)
        rest = x - high.astype(F32)
        middle = rest.astype(BF16)
        low = (rest - middle.astype(F32)).astype(BF16)
        split_ref[n] = jnp.concatenate([high, middle, low, jnp.zeros_like(low)], axis=1)
    for h in range(2):
        sums = branch_sums(wt_ref, h * 128)
        row_ref[:, h * 128 : (h + 1) * 128] = jnp.broadcast_to(sums, (8, 128))
        col_ref[h * 128 : (h + 1) * 128, :] = jnp.broadcast_to(sums, (128, 128)).T


def weigh(counts, totals, lengths):
    return pl.pallas_call(
        weigh_kernel,
        out_shape=(
            jax.ShapeDtypeStruct((KS, ROWS), F32),
            jax.ShapeDtypeStruct((8, KS, 128), BF16),
            jax.ShapeDtypeStruct((8, ROWS), F32),
            jax.ShapeDtypeStruct((ROWS, 128), F32),
        ),
        compiler_params=params(),
        name="weigh",
    )(counts, totals.reshape(1, ROWS), lengths.reshape(1, KS))


def spread_call(name, n_blocks, columns, width, group, mass_row, side=None):
    pairs = group // 2
    halves = 2 if side is None else 1
    groups = halves * ROWS // 2 // group

    def kernel(split_ref, col_ref, *refs):
        blocks = refs[:n_blocks]
        out_ref, pick_ref, even_ref, odd_ref = refs[n_blocks:]
        core = lax.axis_index("branch") % 2
        y = lax.axis_index("blk") // 4
        if side is None:
            base = 0
        else:
            base = (core if side == 0 else 1 - core) * groups

        part = lax.broadcasted_iota(jnp.int32, (128, 256), 0)
        lane = lax.broadcasted_iota(jnp.int32, (128, 256), 1)
        want = jnp.where(part < 96, part % 32 - lane // 128, -1)
        for p in range(16):
            pick_ref[p] = jnp.where(want == 2 * p, 1.0, 0.0).astype(BF16)

        def broadcast_pair(into, g, q, at=slice(0, KS)):
            pair = g * pairs + q
            into[q, at] = jnp.dot(
                split_ref[pair // 16, at], pick_ref[pair % 16], preferred_element_type=F32
            )

        def span(n, lane, at):
            if isinstance(lane, int):
                return blocks[n][at, lane : lane + 128]
            return blocks[n][at, pl.ds(pl.multiple_of(lane, 128), 128)]

        def columns_at(h):
            return columns(h if side is None else base // groups, y)

        for h in range(halves):
            below = [jnp.zeros((1, 128), F32)] * mass_row
            for n, lane in columns_at(h):
                total = jnp.zeros((8, 128), F32)
                for k8 in range(KS // 8):
                    total = total + span(n, lane, slice(k8 * 8, k8 * 8 + 8))
                below.append(jnp.sum(total, axis=0, keepdims=True))
            below += [jnp.zeros((1, 128), F32)] * (8 - len(below))
            out_ref[h, 128:136, 0:128] = jnp.concatenate(below, axis=0)

        for q in range(pairs):
            broadcast_pair(even_ref, base, q)

        def one_group(g, now, later):
            h = g * group // 128
            cols = columns_at(h)
            n_cols = len(cols)
            following = base + jnp.minimum(g + 1, groups - 1)
            steps = []
            if group == 8:
                for q in range(pairs):
                    broadcast_pair(later, following, q)
            else:
                steps = [(q, slice(k, k + 128)) for k in range(0, KS, 128) for q in range(pairs)]
            acc = [jnp.zeros((8, 128), F32)] * (group * n_cols)
            for k8 in range(KS // 8):
                if steps and k8 % 2 == 0:
                    q, at = steps[k8 // 2]
                    broadcast_pair(later, following, q, at)
                at = slice(k8 * 8, k8 * 8 + 8)
                spans = [span(n, lane, at) for n, lane in cols]
                for r in range(group):
                    own = now[r // 2, at, 128 * (r % 2) : 128 * (r % 2) + 128]
                    for j in range(n_cols):
                        acc[r * n_cols + j] += jnp.minimum(own, spans[j])
            for r0 in range(0, group, 8):
                row = pl.multiple_of(g * group + r0 - h * 128, 8)
                first = pl.multiple_of((base + g) * group + r0, 8)
                own_mass = col_ref[pl.ds(first, 8), :]
                for j in range(n_cols):
                    mass = out_ref[h, 128 + mass_row + j : 129 + mass_row + j, 0:128]
                    least = jnp.concatenate(
                        [
                            jnp.sum(acc[(r0 + r) * n_cols + j], axis=0, keepdims=True)
                            for r in range(8)
                        ],
                        axis=0,
                    )
                    out_ref[h, pl.ds(row, 8), 128 * j : 128 * j + 128] = (
                        own_mass + mass - 2.0 * least
                    )

        def two_groups(t, carry):
            one_group(2 * t, even_ref, odd_ref)
            one_group(2 * t + 1, odd_ref, even_ref)
            return carry

        lax.fori_loop(0, groups // 2, two_groups, 0)

    def call(split, col, *blocks):
        return pl.pallas_call(
            kernel,
            out_shape=jax.ShapeDtypeStruct((halves, 136, width), F32),
            in_specs=in_vmem(2 + n_blocks),
            out_specs=in_vmem(1)[0],
            scratch_shapes=[
                pltpu.VMEM((16, 128, 256), BF16),
                pltpu.VMEM((pairs, KS, 256), F32),
                pltpu.VMEM((pairs, KS, 256), F32),
            ],
            compiler_params=params(),
            cost_estimate=pl.CostEstimate(
                flops=halves * width * 128 * KS * 250, bytes_accessed=4 << 20, transcendentals=0
            ),
            name=name,
        )(split, col, *blocks)

    return call


def diagonal_columns(half, y):
    return [(0, 0), (0, 128)]


def first_columns(half, y):
    return [(0, 0), (0, 128), (1, 0), (1, 128)]


def second_columns(half, y):
    return [(0, 0), (0, 128), (1, (half ^ y) * 128)]


def pack_kernel(*refs):
    out_ref = refs[-1]
    core = lax.axis_index("branch") % 2
    lane = 0
    masses = jnp.zeros((8, 128), F32)
    for own, got in zip(refs[:-1:2], refs[1:-1:2], strict=True):
        half = core if own.shape[0] == 2 else 0
        width = own.shape[2]
        both = own[half, 0:128, :] + got[half, 0:128, :]
        out_ref[:, :, lane : lane + width] = both.reshape(16, 8, width)
        masses = masses + own[half, 128:136, 0:128] + got[half, 128:136, 0:128]
        lane += width
    out_ref[:, :, lane:] = jnp.broadcast_to(masses[None], (16, 8, 128))


def pack(*parts):
    width = sum(p.shape[2] for p in parts[::2]) + 128
    return pl.pallas_call(
        pack_kernel,
        out_shape=jax.ShapeDtypeStruct((16, 8, width), F32),
        in_specs=in_vmem(len(parts)),
        out_specs=in_vmem(1)[0],
        compiler_params=params(),
        name="pack",
    )(*parts)


def block_partner(b, slot):
    y, x = b // 4, b % 4
    if slot == 0:
        return b
    if slot == 1:
        return y * 4 + (x + 1) % 4
    if slot == 2:
        return (1 - y) * 4 + (x + 3) % 4
    if slot == 4:
        return (1 - y) * 4 + (x + 2) % 4
    if slot == 5:
        return y * 4 + (x + 3) % 4
    if slot == 6:
        return (1 - y) * 4 + (x + 1) % 4
    far = x // 2
    keep_y = (far == y) if slot == 3 else (far != y)
    return jnp.where(keep_y, y * 4 + (x + 2) % 4, (1 - y) * 4 + x)


def assemble_kernel(own1, other1, own2, other2, out_ref, turned_ref, sems):
    core = lax.axis_index("branch") % 2
    b = lax.axis_index("blk")
    y = b // 4
    stores = []

    def store(src, rows, cols):
        copy = pltpu.make_async_copy(src, out_ref.at[rows, cols], sems.at[len(stores)])
        copy.start()
        stores.append(copy)

    def rows_of(half):
        return pl.ds(pl.multiple_of(half * 128, 128), 128)

    def columns(slot, half=None):
        first = block_partner(b, slot) * ROWS
        if half is None:
            return pl.ds(pl.multiple_of(first, ROWS), ROWS)
        return pl.ds(pl.multiple_of(first + half * 128, 128), 128)

    both = ((0, core, own1, own2), (1, 1 - core, other1, other2))
    for _, half, ref1, ref2 in both:
        rows = rows_of(half)
        for slot, ref, lane in ((0, ref1, 0), (1, ref1, 256), (2, ref1, 512), (3, ref2, 0)):
            store(ref.at[:, lane : lane + ROWS], rows, columns(slot))
        store(ref2.at[:, 256:384], rows, columns(4, half ^ y))
    for side, half, ref1, ref2 in both:
        for n, (slot, ref, lane) in enumerate(((5, ref1, 768), (6, ref1, 1024), (7, ref2, 384))):
            turned_ref[side, n] = ref[:, lane : lane + ROWS].T
            store(turned_ref.at[side, n], slice(0, ROWS), columns(slot, half))
        turned_ref[side, 3, 0:128] = ref2[:, 640:768].T
        store(turned_ref.at[side, 3, 0:128], rows_of(half ^ (1 - y)), columns(4, half))
    for copy in stores:
        copy.wait()


def assemble(*pieces):
    return pl.pallas_call(
        assemble_kernel,
        out_shape=jax.ShapeDtypeStruct((ROWS, BLOCKS * ROWS), F32),
        in_specs=in_vmem(4),
        out_specs=pl.BlockSpec(memory_space=pl.ANY),
        scratch_shapes=[
            pltpu.VMEM((2, 4, ROWS, 128), F32),
            pltpu.SemaphoreType.DMA((18,)),
        ],
        compiler_params=params(),
        name="assemble",
    )(*[p.reshape(128, p.shape[2]) for p in pieces])


def on_device(counts, totals, lengths):
    branch = lax.axis_index("branch")
    place = branch // 2

    def from_partner(v, n):
        return lax.ppermute(v, "blk", [(PARTNERS[n][b], b) for b in range(BLOCKS)])

    def to_partner(v, n):
        return lax.ppermute(v, "blk", [(b, PARTNERS[n][b]) for b in range(BLOCKS)])

    def other_core(v):
        return lax.ppermute(v, "branch", [(i, i ^ 1) for i in range(32)])

    chips = [[2 * p + c for p in range(16)] for c in range(2)]

    def over_chips(v):
        return lax.all_to_all(v, "branch", 0, 0, axis_index_groups=chips)

    def gather(pieces):
        mine = jnp.concatenate(pieces, axis=1)
        whole = over_chips(jnp.broadcast_to(mine[None], (16, *mine.shape)))
        return whole, other_core(whole)

    def tied(v, *others):
        return lax.optimization_barrier((v, *others))[0]

    wt, split, mass_row, mass_col = weigh(counts, totals, lengths)
    got = [from_partner(wt, n) for n in range(2)]
    diagonal = spread_call("diagonal", 1, diagonal_columns, 256, 16, 0)
    first = [spread_call(f"first{s}", 2, first_columns, 512, 8, 2, s) for s in range(2)]
    second = [spread_call(f"second{s}", 2, second_columns, 384, 8, 0, s) for s in range(2)]

    part0 = diagonal(split, mass_col, wt)
    later = tied(wt, part0)
    got += [from_partner(later, n) for n in (2, 3)]
    received0 = other_core(part0)
    received1 = other_core(first[1](split, mass_col, got[0], got[1]))
    kept1 = first[0](split, mass_col, got[0], got[1])
    payload1 = pack(part0, received0, kept1, received1)
    shard = jnp.sum(over_chips(payload1), axis=0)

    third = tied(got[2], payload1)
    received2 = other_core(second[1](split, mass_col, third, got[3]))

    mass = shard[:, 768:]
    own_half = jnp.where(branch % 2 == 0, mass[0], mass[1])
    own_mass = lax.dynamic_slice_in_dim(own_half, place * 8, 8)[:, None]
    dist1 = shard[:, :768] / (own_mass + mass[0:6].reshape(768)[None, :])
    swapped1 = [to_partner(dist1[:, 256 * (n + 1) : 256 * (n + 2)], n) for n in range(2)]

    third = tied(third, dist1, received2)
    kept2 = second[0](split, mass_col, third, got[3])
    payload2 = pack(kept2, received2)
    shard = jnp.sum(over_chips(payload2), axis=0)
    dist2 = shard[:, :384] / (own_mass + shard[0:3, 384:].reshape(384)[None, :])
    swapped2 = [to_partner(dist2[:, 0:256], 2), to_partner(dist2[:, 256:384], 3)]

    own1, other1 = gather([tied(dist1, payload2), *swapped1])
    own2, other2 = gather([dist2, *swapped2])
    return assemble(own1, other1, own2, other2)


def solution(mesh):
    placed = (P("blk", "branch"), P("blk"), P("branch"))
    return jax.shard_map(
        on_device, mesh=mesh, in_specs=placed, out_specs=P("blk", None), check_vma=False
    )
```

```python
import jax
import jax.numpy as jnp
from jax import lax
from jax.experimental import pallas as pl
from jax.experimental.pallas import tpu as pltpu
from jax.sharding import PartitionSpec as P

F32 = jnp.float32
BF16 = jnp.bfloat16
ROWS = 256
KS = 512
BLOCKS = 8
GROUP = 8
PAIRS = GROUP // 2
GROUPS = ROWS // GROUP


def block_at(y, x):
    return (y % 2) * 4 + x % 4


def partner_tables():
    first, second, third, fourth = [], [], [], []
    for b in range(BLOCKS):
        y, x = b // 4, b % 4
        first.append(block_at(y, x + 1))
        second.append(block_at(y + 1, x + 3))
        cycle = {(0, 0): (0, 2), (0, 1): (1, 2), (1, 1): (1, 0), (1, 0): (0, 0)}
        ny, nx = cycle[(y, x // 2)]
        third.append(block_at(ny, nx + x % 2))
        fourth.append(block_at(y + 1, x + 2))
    return [first, second, third, fourth]


PARTNERS = partner_tables()
OWNERS = [[table.index(b) for b in range(BLOCKS)] for table in PARTNERS]


def params():
    return pltpu.CompilerParams(vmem_limit_bytes=24 << 20)


def in_vmem(n):
    return [pl.BlockSpec(memory_space=pltpu.VMEM)] * n


def branch_sums(ref, lane):
    def add(k8, total):
        at = pl.ds(pl.multiple_of(k8 * 8, 8), 8)
        return total + ref[at, lane : lane + 128]

    total = lax.fori_loop(0, KS // 8, add, jnp.zeros((8, 128), F32), unroll=8)
    return jnp.sum(total, axis=0, keepdims=True)


def weigh_kernel(counts_hbm, totals_hbm, lengths_hbm, wt_ref, split_ref, col_ref, *scratch):
    counts_ref, totals_ref, lengths_ref, sems = scratch
    loads = [
        pltpu.make_async_copy(src, dst, sems.at[n])
        for n, (src, dst) in enumerate(
            ((counts_hbm, counts_ref), (totals_hbm, totals_ref), (lengths_hbm, lengths_ref))
        )
    ]
    for load in loads:
        load.start()
    for load in loads:
        load.wait()
    scaled = lengths_ref[...].astype(F32) * 0.001
    wt = (scaled * counts_ref[...].astype(F32)).T / totals_ref[...].astype(F32)
    wt_ref[...] = wt
    for n in range(8):
        x = wt[:, n * 32 : (n + 1) * 32]
        high = x.astype(BF16)
        rest = x - high.astype(F32)
        middle = rest.astype(BF16)
        low = (rest - middle.astype(F32)).astype(BF16)
        split_ref[n] = jnp.concatenate([high, middle, low, jnp.zeros_like(low)], axis=1)
    for h in range(2):
        sums = branch_sums(wt_ref, h * 128)
        col_ref[h * 128 : (h + 1) * 128, :] = jnp.broadcast_to(sums, (128, 128)).T


def weigh(counts, totals, lengths):
    return pl.pallas_call(
        weigh_kernel,
        out_shape=(
            jax.ShapeDtypeStruct((KS, ROWS), F32),
            jax.ShapeDtypeStruct((8, KS, 128), BF16),
            jax.ShapeDtypeStruct((ROWS, 128), F32),
        ),
        in_specs=[pl.BlockSpec(memory_space=pltpu.HBM)] * 3,
        out_specs=tuple(in_vmem(3)),
        scratch_shapes=[
            pltpu.VMEM((ROWS, KS), jnp.int32),
            pltpu.VMEM((1, ROWS), jnp.int32),
            pltpu.VMEM((1, KS), jnp.int32),
            pltpu.SemaphoreType.DMA((3,)),
        ],
        compiler_params=params(),
        name="weigh",
    )(counts, totals.reshape(1, ROWS), lengths.reshape(1, KS))


def spread_call(name, n_blocks, columns, width, group, mass_row, side=None):
    pairs = group // 2
    halves = 2 if side is None else 1
    groups = halves * ROWS // 2 // group

    def kernel(split_ref, col_ref, *refs):
        blocks = refs[:n_blocks]
        out_ref, pick_ref, even_ref, odd_ref = refs[n_blocks:]
        core = lax.axis_index("branch") % 2
        y = lax.axis_index("blk") // 4
        if side is None:
            base = 0
        else:
            base = (core if side == 0 else 1 - core) * groups

        part = lax.broadcasted_iota(jnp.int32, (128, 256), 0)
        lane = lax.broadcasted_iota(jnp.int32, (128, 256), 1)
        want = jnp.where(part < 96, part % 32 - lane // 128, -1)
        for p in range(16):
            pick_ref[p] = jnp.where(want == 2 * p, 1.0, 0.0).astype(BF16)

        def broadcast_pair(into, g, q, at=slice(0, KS)):
            pair = g * pairs + q
            into[q, at] = jnp.dot(
                split_ref[pair // 16, at], pick_ref[pair % 16], preferred_element_type=F32
            )

        def span(n, lane, at):
            if isinstance(lane, int):
                return blocks[n][at, lane : lane + 128]
            return blocks[n][at, pl.ds(pl.multiple_of(lane, 128), 128)]

        def columns_at(h):
            return columns(h if side is None else base // groups, y)

        for h in range(halves):
            below = [jnp.zeros((1, 128), F32)] * mass_row
            for n, lane in columns_at(h):
                total = jnp.zeros((8, 128), F32)
                for k8 in range(KS // 8):
                    total = total + span(n, lane, slice(k8 * 8, k8 * 8 + 8))
                below.append(jnp.sum(total, axis=0, keepdims=True))
            below += [jnp.zeros((1, 128), F32)] * (8 - len(below))
            out_ref[h, 128:136, 0:128] = jnp.concatenate(below, axis=0)

        for q in range(pairs):
            broadcast_pair(even_ref, base, q)

        def one_group(g, now, later):
            h = g * group // 128
            cols = columns_at(h)
            n_cols = len(cols)
            following = base + jnp.minimum(g + 1, groups - 1)
            steps = []
            if group == 8:
                for q in range(pairs):
                    broadcast_pair(later, following, q)
            else:
                steps = [(q, slice(k, k + 128)) for k in range(0, KS, 128) for q in range(pairs)]
            acc = [jnp.zeros((8, 128), F32)] * (group * n_cols)
            for k8 in range(KS // 8):
                if steps and k8 % 2 == 0:
                    q, at = steps[k8 // 2]
                    broadcast_pair(later, following, q, at)
                at = slice(k8 * 8, k8 * 8 + 8)
                spans = [span(n, lane, at) for n, lane in cols]
                for r in range(group):
                    own = now[r // 2, at, 128 * (r % 2) : 128 * (r % 2) + 128]
                    for j in range(n_cols):
                        acc[r * n_cols + j] += jnp.minimum(own, spans[j])
            for r0 in range(0, group, 8):
                row = pl.multiple_of(g * group + r0 - h * 128, 8)
                first = pl.multiple_of((base + g) * group + r0, 8)
                own_mass = col_ref[pl.ds(first, 8), :]
                for j in range(n_cols):
                    mass = out_ref[h, 128 + mass_row + j : 129 + mass_row + j, 0:128]
                    least = jnp.concatenate(
                        [
                            jnp.sum(acc[(r0 + r) * n_cols + j], axis=0, keepdims=True)
                            for r in range(8)
                        ],
                        axis=0,
                    )
                    out_ref[h, pl.ds(row, 8), 128 * j : 128 * j + 128] = (
                        own_mass + mass - 2.0 * least
                    )

        def two_groups(t, carry):
            one_group(2 * t, even_ref, odd_ref)
            one_group(2 * t + 1, odd_ref, even_ref)
            return carry

        lax.fori_loop(0, groups // 2, two_groups, 0)

    def call(split, col, *blocks):
        return pl.pallas_call(
            kernel,
            out_shape=jax.ShapeDtypeStruct((halves, 136, width), F32),
            in_specs=in_vmem(2 + n_blocks),
            out_specs=in_vmem(1)[0],
            scratch_shapes=[
                pltpu.VMEM((16, 128, 256), BF16),
                pltpu.VMEM((pairs, KS, 256), F32),
                pltpu.VMEM((pairs, KS, 256), F32),
            ],
            compiler_params=params(),
            cost_estimate=pl.CostEstimate(
                flops=halves * width * 128 * KS * 250, bytes_accessed=4 << 20, transcendentals=0
            ),
            name=name,
        )(split, col, *blocks)

    return call


def diagonal_columns(half, y):
    return [(0, 0), (0, 128)]


def first_columns(half, y):
    return [(0, 0), (0, 128), (1, 0), (1, 128)]


def second_columns(half, y):
    return [(0, 0), (0, 128), (1, (half ^ y) * 128)]


def pack_kernel(*refs):
    out_ref = refs[-1]
    core = lax.axis_index("branch") % 2
    lane = 0
    masses = jnp.zeros((8, 128), F32)
    for own, got in zip(refs[:-1:2], refs[1:-1:2], strict=True):
        half = core if own.shape[0] == 2 else 0
        width = own.shape[2]
        both = own[half, 0:128, :] + got[half, 0:128, :]
        out_ref[:, :, lane : lane + width] = both.reshape(16, 8, width)
        masses = masses + own[half, 128:136, 0:128] + got[half, 128:136, 0:128]
        lane += width
    out_ref[:, :, lane:] = jnp.broadcast_to(masses[None], (16, 8, 128))


def pack(*parts):
    width = sum(p.shape[2] for p in parts[::2]) + 128
    return pl.pallas_call(
        pack_kernel,
        out_shape=jax.ShapeDtypeStruct((16, 8, width), F32),
        in_specs=in_vmem(len(parts)),
        out_specs=in_vmem(1)[0],
        compiler_params=params(),
        name="pack",
    )(*parts)


def block_partner(b, slot):
    y, x = b // 4, b % 4
    if slot == 0:
        return b
    if slot == 1:
        return y * 4 + (x + 1) % 4
    if slot == 2:
        return (1 - y) * 4 + (x + 3) % 4
    if slot == 4:
        return (1 - y) * 4 + (x + 2) % 4
    if slot == 5:
        return y * 4 + (x + 3) % 4
    if slot == 6:
        return (1 - y) * 4 + (x + 1) % 4
    far = x // 2
    keep_y = (far == y) if slot == 3 else (far != y)
    return jnp.where(keep_y, y * 4 + (x + 2) % 4, (1 - y) * 4 + x)


def assemble_kernel(own, other, out_ref, turned_ref, sems):
    core = lax.axis_index("branch") % 2
    b = lax.axis_index("blk")
    y = b // 4
    stores = []

    def store(src, rows, cols):
        copy = pltpu.make_async_copy(src, out_ref.at[rows, cols], sems.at[len(stores)])
        copy.start()
        stores.append(copy)

    def rows_of(half):
        return pl.ds(pl.multiple_of(half * 128, 128), 128)

    def columns(slot, half=None):
        first = block_partner(b, slot) * ROWS
        if half is None:
            return pl.ds(pl.multiple_of(first, ROWS), ROWS)
        return pl.ds(pl.multiple_of(first + half * 128, 128), 128)

    both = ((0, core, own), (1, 1 - core, other))
    for _, half, ref in both:
        rows = rows_of(half)
        for slot, lane in ((0, 0), (1, 256), (2, 512), (3, 768)):
            store(ref.at[:, lane : lane + ROWS], rows, columns(slot))
        store(ref.at[:, 1024:1152], rows, columns(4, half ^ y))
    for side, half, ref in both:
        for n, slot in enumerate((5, 6, 7)):
            lane = 1152 + n * ROWS
            turned_ref[side, n] = ref[:, lane : lane + ROWS].T
            store(turned_ref.at[side, n], slice(0, ROWS), columns(slot, half))
        turned_ref[side, 3, 0:128] = ref[:, 1920:2048].T
        store(turned_ref.at[side, 3, 0:128], rows_of(half ^ (1 - y)), columns(4, half))
    for copy in stores:
        copy.wait()


def assemble(*pieces):
    return pl.pallas_call(
        assemble_kernel,
        out_shape=jax.ShapeDtypeStruct((ROWS, BLOCKS * ROWS), F32),
        in_specs=in_vmem(2),
        out_specs=pl.BlockSpec(memory_space=pl.ANY),
        scratch_shapes=[
            pltpu.VMEM((2, 4, ROWS, 128), F32),
            pltpu.SemaphoreType.DMA((18,)),
        ],
        compiler_params=params(),
        name="assemble",
    )(*[p.reshape(128, p.shape[2]) for p in pieces])


def on_device(counts, totals, lengths):
    branch = lax.axis_index("branch")
    place = branch // 2

    def from_partner(v, n):
        return lax.ppermute(v, "blk", [(PARTNERS[n][b], b) for b in range(BLOCKS)])

    def to_partner(v, n):
        return lax.ppermute(v, "blk", [(b, PARTNERS[n][b]) for b in range(BLOCKS)])

    def other_core(v):
        return lax.ppermute(v, "branch", [(i, i ^ 1) for i in range(32)])

    chips = [[2 * p + c for p in range(16)] for c in range(2)]

    def over_chips(v):
        return lax.all_to_all(v, "branch", 0, 0, axis_index_groups=chips)

    def gather(pieces):
        mine = jnp.concatenate(pieces, axis=1)
        whole = over_chips(jnp.broadcast_to(mine[None], (16, *mine.shape)))
        return whole, other_core(whole)

    def tied(v, *others):
        return lax.optimization_barrier((v, *others))[0]

    wt, split, mass_col = weigh(counts, totals, lengths)
    got = [from_partner(wt, n) for n in range(2)]
    diagonal = spread_call("diagonal", 1, diagonal_columns, 256, 16, 0)
    first = [spread_call(f"first{s}", 2, first_columns, 512, 8, 2, s) for s in range(2)]
    second = [spread_call(f"second{s}", 2, second_columns, 384, 8, 0, s) for s in range(2)]

    part0 = diagonal(split, mass_col, wt)
    later = tied(wt, part0)
    got += [from_partner(later, n) for n in (2, 3)]
    received0 = other_core(part0)
    received1 = other_core(first[1](split, mass_col, got[0], got[1]))
    kept1 = first[0](split, mass_col, got[0], got[1])
    payload1 = pack(part0, received0, kept1, received1)
    shard = jnp.sum(over_chips(payload1), axis=0)

    third = tied(got[2], payload1)
    received2 = other_core(second[1](split, mass_col, third, got[3]))

    mass = shard[:, 768:]
    own_half = jnp.where(branch % 2 == 0, mass[0], mass[1])
    own_mass = lax.dynamic_slice_in_dim(own_half, place * 8, 8)[:, None]
    dist1 = shard[:, :768] / (own_mass + mass[0:6].reshape(768)[None, :])
    swapped1 = [to_partner(dist1[:, 256 * (n + 1) : 256 * (n + 2)], n) for n in range(2)]

    third = tied(third, dist1, received2)
    kept2 = second[0](split, mass_col, third, got[3])
    payload2 = pack(tied(kept2, *swapped1), received2)
    shard = jnp.sum(over_chips(payload2), axis=0)
    dist2 = shard[:, :384] / (own_mass + shard[0:3, 384:].reshape(384)[None, :])
    swapped2 = [to_partner(dist2[:, 0:256], 2), to_partner(dist2[:, 256:384], 3)]

    return assemble(*gather([dist1, dist2, *swapped1, *swapped2]))


def solution(mesh):
    placed = (P("blk", "branch"), P("blk"), P("branch"))
    return jax.shard_map(
        on_device, mesh=mesh, in_specs=placed, out_specs=P("blk", None), check_vma=False
    )
```

```python
import jax
import jax.numpy as jnp
from jax import lax
from jax.experimental import pallas as pl
from jax.experimental.pallas import tpu as pltpu
from jax.sharding import PartitionSpec as P

F32 = jnp.float32
BF16 = jnp.bfloat16
ROWS = 256
KS = 512
BLOCKS = 8
GROUP = 8
PAIRS = GROUP // 2
GROUPS = ROWS // GROUP


def block_at(y, x):
    return (y % 2) * 4 + x % 4


def partner_tables():
    first, second, third, fourth = [], [], [], []
    for b in range(BLOCKS):
        y, x = b // 4, b % 4
        first.append(block_at(y, x + 1))
        second.append(block_at(y + 1, x + 3))
        cycle = {(0, 0): (0, 2), (0, 1): (1, 2), (1, 1): (1, 0), (1, 0): (0, 0)}
        ny, nx = cycle[(y, x // 2)]
        third.append(block_at(ny, nx + x % 2))
        fourth.append(block_at(y + 1, x + 2))
    return [first, second, third, fourth]


PARTNERS = partner_tables()


def params():
    return pltpu.CompilerParams(vmem_limit_bytes=24 << 20)


def in_vmem(n):
    return [pl.BlockSpec(memory_space=pltpu.VMEM)] * n


def branch_sums(ref, lane):
    def add(k8, total):
        at = pl.ds(pl.multiple_of(k8 * 8, 8), 8)
        return total + ref[at, lane : lane + 128]

    total = lax.fori_loop(0, KS // 8, add, jnp.zeros((8, 128), F32), unroll=8)
    return jnp.sum(total, axis=0, keepdims=True)


def weigh_kernel(counts_hbm, totals_hbm, lengths_hbm, wt_ref, split_ref, col_ref, *scratch):
    counts_ref, totals_ref, lengths_ref, sems = scratch
    loads = [
        pltpu.make_async_copy(src, dst, sems.at[n])
        for n, (src, dst) in enumerate(
            ((counts_hbm, counts_ref), (totals_hbm, totals_ref), (lengths_hbm, lengths_ref))
        )
    ]
    for load in loads:
        load.start()
    for load in loads:
        load.wait()
    scaled = lengths_ref[...].astype(F32) * 0.001
    wt = (scaled * counts_ref[...].astype(F32)).T / totals_ref[...].astype(F32)
    wt_ref[...] = wt
    for n in range(8):
        x = wt[:, n * 32 : (n + 1) * 32]
        high = x.astype(BF16)
        rest = x - high.astype(F32)
        middle = rest.astype(BF16)
        low = (rest - middle.astype(F32)).astype(BF16)
        split_ref[n] = jnp.concatenate([high, middle, low, jnp.zeros_like(low)], axis=1)
    for h in range(2):
        sums = branch_sums(wt_ref, h * 128)
        col_ref[h * 128 : (h + 1) * 128, :] = jnp.broadcast_to(sums, (128, 128)).T


def weigh(counts, totals, lengths):
    return pl.pallas_call(
        weigh_kernel,
        out_shape=(
            jax.ShapeDtypeStruct((KS, ROWS), F32),
            jax.ShapeDtypeStruct((8, KS, 128), BF16),
            jax.ShapeDtypeStruct((ROWS, 128), F32),
        ),
        in_specs=[pl.BlockSpec(memory_space=pltpu.HBM)] * 3,
        out_specs=tuple(in_vmem(3)),
        scratch_shapes=[
            pltpu.VMEM((ROWS, KS), jnp.int32),
            pltpu.VMEM((1, ROWS), jnp.int32),
            pltpu.VMEM((1, KS), jnp.int32),
            pltpu.SemaphoreType.DMA((3,)),
        ],
        compiler_params=params(),
        name="weigh",
    )(counts, totals.reshape(1, ROWS), lengths.reshape(1, KS))


def spread_call(name, n_blocks, columns, width, group, mass_row, side=None):
    pairs = group // 2
    halves = 2 if side is None else 1
    groups = halves * ROWS // 2 // group

    def kernel(split_ref, col_ref, *refs):
        blocks = refs[:n_blocks]
        out_ref, pick_ref, even_ref, odd_ref = refs[n_blocks:]
        core = lax.axis_index("branch") % 2
        y = lax.axis_index("blk") // 4
        if side is None:
            base = 0
        else:
            base = (core if side == 0 else 1 - core) * groups

        part = lax.broadcasted_iota(jnp.int32, (128, 256), 0)
        lane = lax.broadcasted_iota(jnp.int32, (128, 256), 1)
        want = jnp.where(part < 96, part % 32 - lane // 128, -1)
        for p in range(16):
            pick_ref[p] = jnp.where(want == 2 * p, 1.0, 0.0).astype(BF16)

        def broadcast_pair(into, g, q, at=slice(0, KS)):
            pair = g * pairs + q
            into[q, at] = jnp.dot(
                split_ref[pair // 16, at], pick_ref[pair % 16], preferred_element_type=F32
            )

        def span(n, lane, at):
            if isinstance(lane, int):
                return blocks[n][at, lane : lane + 128]
            return blocks[n][at, pl.ds(pl.multiple_of(lane, 128), 128)]

        def columns_at(h):
            return columns(h if side is None else base // groups, y)

        for h in range(halves):
            below = [jnp.zeros((1, 128), F32)] * mass_row
            for n, lane in columns_at(h):
                total = jnp.zeros((8, 128), F32)
                for k8 in range(KS // 8):
                    total = total + span(n, lane, slice(k8 * 8, k8 * 8 + 8))
                below.append(jnp.sum(total, axis=0, keepdims=True))
            below += [jnp.zeros((1, 128), F32)] * (8 - len(below))
            out_ref[h, 128:136, 0:128] = jnp.concatenate(below, axis=0)

        for q in range(pairs):
            broadcast_pair(even_ref, base, q)

        def one_group(g, now, later):
            h = g * group // 128
            cols = columns_at(h)
            n_cols = len(cols)
            following = base + jnp.minimum(g + 1, groups - 1)
            steps = []
            if group == 8:
                for q in range(pairs):
                    broadcast_pair(later, following, q)
            else:
                steps = [(q, slice(k, k + 128)) for k in range(0, KS, 128) for q in range(pairs)]
            acc = [jnp.zeros((8, 128), F32)] * (group * n_cols)
            for k8 in range(KS // 8):
                if steps and k8 % 2 == 0:
                    q, at = steps[k8 // 2]
                    broadcast_pair(later, following, q, at)
                at = slice(k8 * 8, k8 * 8 + 8)
                spans = [span(n, lane, at) for n, lane in cols]
                for r in range(group):
                    own = now[r // 2, at, 128 * (r % 2) : 128 * (r % 2) + 128]
                    for j in range(n_cols):
                        acc[r * n_cols + j] += jnp.minimum(own, spans[j])
            for r0 in range(0, group, 8):
                row = pl.multiple_of(g * group + r0 - h * 128, 8)
                first = pl.multiple_of((base + g) * group + r0, 8)
                own_mass = col_ref[pl.ds(first, 8), :]
                for j in range(n_cols):
                    mass = out_ref[h, 128 + mass_row + j : 129 + mass_row + j, 0:128]
                    least = jnp.concatenate(
                        [
                            jnp.sum(acc[(r0 + r) * n_cols + j], axis=0, keepdims=True)
                            for r in range(8)
                        ],
                        axis=0,
                    )
                    out_ref[h, pl.ds(row, 8), 128 * j : 128 * j + 128] = (
                        own_mass + mass - 2.0 * least
                    )

        def two_groups(t, carry):
            one_group(2 * t, even_ref, odd_ref)
            one_group(2 * t + 1, odd_ref, even_ref)
            return carry

        lax.fori_loop(0, groups // 2, two_groups, 0)

    def call(split, col, *blocks):
        return pl.pallas_call(
            kernel,
            out_shape=jax.ShapeDtypeStruct((halves, 136, width), F32),
            in_specs=in_vmem(2 + n_blocks),
            out_specs=in_vmem(1)[0],
            scratch_shapes=[
                pltpu.VMEM((16, 128, 256), BF16),
                pltpu.VMEM((pairs, KS, 256), F32),
                pltpu.VMEM((pairs, KS, 256), F32),
            ],
            compiler_params=params(),
            cost_estimate=pl.CostEstimate(
                flops=halves * width * 128 * KS * 250, bytes_accessed=4 << 20, transcendentals=0
            ),
            name=name,
        )(split, col, *blocks)

    return call


def diagonal_columns(half, y):
    return [(0, 0), (0, 128)]


def first_columns(half, y):
    return [(0, 0), (0, 128), (1, 0), (1, 128)]


def second_columns(half, y):
    return [(0, 0), (0, 128), (1, (half ^ y) * 128)]


DIRECT = 1152


def pack_kernel(own0, got0, own1, got1, own2, got2, out_ref):
    core = lax.axis_index("branch") % 2
    lane = 0
    masses = []
    for own, got in ((own0, got0), (own1, got1), (own2, got2)):
        half = core if own.shape[0] == 2 else 0
        width = own.shape[2]
        both = own[half, 0:128, :] + got[half, 0:128, :]
        out_ref[:, :, lane : lane + width] = both.reshape(16, 8, width)
        masses.append(own[half, 128:136, 0:128] + got[half, 128:136, 0:128])
        lane += width
    for block in (masses[0] + masses[1], masses[2]):
        out_ref[:, :, lane : lane + 128] = jnp.broadcast_to(block[None], (16, 8, 128))
        lane += 128


def pack(*parts):
    return pl.pallas_call(
        pack_kernel,
        out_shape=jax.ShapeDtypeStruct((16, 8, DIRECT + 256), F32),
        in_specs=in_vmem(6),
        out_specs=in_vmem(1)[0],
        compiler_params=params(),
        name="pack",
    )(*parts)


def block_partner(b, slot):
    y, x = b // 4, b % 4
    if slot == 0:
        return b
    if slot == 1:
        return y * 4 + (x + 1) % 4
    if slot == 2:
        return (1 - y) * 4 + (x + 3) % 4
    if slot == 4:
        return (1 - y) * 4 + (x + 2) % 4
    if slot == 5:
        return y * 4 + (x + 3) % 4
    if slot == 6:
        return (1 - y) * 4 + (x + 1) % 4
    far = x // 2
    keep_y = (far == y) if slot == 3 else (far != y)
    return jnp.where(keep_y, y * 4 + (x + 2) % 4, (1 - y) * 4 + x)


def normalise_kernel(shards_ref, dist_ref, swap_ref):
    branch = lax.axis_index("branch")
    b = lax.axis_index("blk")
    core, place = branch % 2, branch // 2
    total = jnp.sum(shards_ref[...], axis=0)
    rows = [total[r : r + 1, DIRECT : DIRECT + 128] for r in range(6)]
    rows += [total[r : r + 1, DIRECT + 128 : DIRECT + 256] for r in range(3)]
    mine = jnp.broadcast_to(jnp.where(core == 0, rows[0], rows[1]), (8, 128))
    lane = lax.broadcasted_iota(jnp.int32, (8, 128), 1)
    row = lax.broadcasted_iota(jnp.int32, (8, 128), 0)
    own = jnp.sum(jnp.where(lane == place * 8 + row, mine, 0.0), axis=1, keepdims=True)
    for j in range(DIRECT // 128):
        at = slice(128 * j, 128 * j + 128)
        dist_ref[:, at] = total[:, at] / (own + rows[j])
    swap_ref[...] = jnp.zeros_like(swap_ref)
    for slot in range(1, 4):
        swap_ref[block_partner(b, slot)] = dist_ref[:, slot * ROWS : (slot + 1) * ROWS]
    swap_ref[block_partner(b, 4), :, 0:128] = dist_ref[:, 4 * ROWS : DIRECT]


def normalise(shards):
    return pl.pallas_call(
        normalise_kernel,
        out_shape=(
            jax.ShapeDtypeStruct((8, DIRECT), F32),
            jax.ShapeDtypeStruct((BLOCKS, 8, ROWS), F32),
        ),
        in_specs=in_vmem(1),
        out_specs=tuple(in_vmem(2)),
        compiler_params=params(),
        name="normalise",
    )(shards)


def spread_out_kernel(dist_ref, swapped_ref, out_ref):
    b = lax.axis_index("blk")
    pieces = [dist_ref[...]]
    pieces += [swapped_ref[block_partner(b, slot)] for slot in (5, 6, 7)]
    pieces.append(swapped_ref[block_partner(b, 4), :, 0:128])
    whole = jnp.concatenate(pieces, axis=1)
    out_ref[...] = jnp.broadcast_to(whole[None], out_ref.shape)


def spread_out(dist, swapped):
    return pl.pallas_call(
        spread_out_kernel,
        out_shape=jax.ShapeDtypeStruct((16, 8, BLOCKS * ROWS), F32),
        in_specs=in_vmem(2),
        out_specs=in_vmem(1)[0],
        compiler_params=params(),
        name="spread_out",
    )(dist, swapped)


def assemble_kernel(own, other, out_ref, turned_ref, sems):
    core = lax.axis_index("branch") % 2
    b = lax.axis_index("blk")
    y = b // 4
    stores = []

    def store(src, rows, cols):
        copy = pltpu.make_async_copy(src, out_ref.at[rows, cols], sems.at[len(stores)])
        copy.start()
        stores.append(copy)

    def rows_of(half):
        return pl.ds(pl.multiple_of(half * 128, 128), 128)

    def columns(slot, half=None):
        first = block_partner(b, slot) * ROWS
        if half is None:
            return pl.ds(pl.multiple_of(first, ROWS), ROWS)
        return pl.ds(pl.multiple_of(first + half * 128, 128), 128)

    both = ((0, core, own), (1, 1 - core, other))
    for _, half, ref in both:
        rows = rows_of(half)
        for slot, lane in ((0, 0), (1, 256), (2, 512), (3, 768)):
            store(ref.at[:, lane : lane + ROWS], rows, columns(slot))
        store(ref.at[:, 1024:1152], rows, columns(4, half ^ y))
    for side, half, ref in both:
        for n, slot in enumerate((5, 6, 7)):
            lane = 1152 + n * ROWS
            turned_ref[side, n] = ref[:, lane : lane + ROWS].T
            store(turned_ref.at[side, n], slice(0, ROWS), columns(slot, half))
        turned_ref[side, 3, 0:128] = ref[:, 1920:2048].T
        store(turned_ref.at[side, 3, 0:128], rows_of(half ^ (1 - y)), columns(4, half))
    for copy in stores:
        copy.wait()


def assemble(*pieces):
    return pl.pallas_call(
        assemble_kernel,
        out_shape=jax.ShapeDtypeStruct((ROWS, BLOCKS * ROWS), F32),
        in_specs=in_vmem(2),
        out_specs=pl.BlockSpec(memory_space=pl.ANY),
        scratch_shapes=[
            pltpu.VMEM((2, 4, ROWS, 128), F32),
            pltpu.SemaphoreType.DMA((18,)),
        ],
        compiler_params=params(),
        name="assemble",
    )(*[p.reshape(128, p.shape[2]) for p in pieces])


def on_device(counts, totals, lengths):
    def from_partner(v, n):
        return lax.ppermute(v, "blk", [(PARTNERS[n][b], b) for b in range(BLOCKS)])

    def other_core(v):
        return lax.ppermute(v, "branch", [(i, i ^ 1) for i in range(32)])

    chips = [[2 * p + c for p in range(16)] for c in range(2)]

    def over_chips(v):
        return lax.all_to_all(v, "branch", 0, 0, axis_index_groups=chips)

    wt, split, mass_col = weigh(counts, totals, lengths)
    got = [from_partner(wt, n) for n in range(2)]
    diagonal = spread_call("diagonal", 1, diagonal_columns, 256, 16, 0)
    first = spread_call("first", 2, first_columns, 512, 8, 2)
    second = [spread_call(f"second{s}", 2, second_columns, 384, 8, 0, s) for s in range(2)]

    part0 = diagonal(split, mass_col, wt)
    later = lax.optimization_barrier((wt, part0))[0]
    got += [from_partner(later, n) for n in (2, 3)]
    received0 = other_core(part0)
    part1 = first(split, mass_col, got[0], got[1])
    received1 = other_core(part1)
    third = lax.optimization_barrier((got[2], part1))[0]
    sent2 = second[1](split, mass_col, third, got[3])
    received2 = other_core(sent2)
    third = lax.optimization_barrier((third, sent2))[0]
    part2 = second[0](split, mass_col, third, got[3])

    shards = over_chips(pack(part0, received0, part1, received1, part2, received2))
    dist, swap = normalise(shards)
    whole = over_chips(spread_out(dist, lax.all_to_all(swap, "blk", 0, 0)))
    return assemble(whole, other_core(whole))


def solution(mesh):
    placed = (P("blk", "branch"), P("blk"), P("branch"))
    return jax.shard_map(
        on_device, mesh=mesh, in_specs=placed, out_specs=P("blk", None), check_vma=False
    )
```

```python
import jax
import jax.numpy as jnp
from jax import lax
from jax.experimental import pallas as pl
from jax.experimental.pallas import tpu as pltpu
from jax.sharding import PartitionSpec as P

F32 = jnp.float32
BF16 = jnp.bfloat16
ROWS = 256
KS = 512
BLOCKS = 8
GROUP = 8
PAIRS = GROUP // 2
GROUPS = ROWS // GROUP


def block_at(y, x):
    return (y % 2) * 4 + x % 4


def partner_tables():
    first, second, third, fourth = [], [], [], []
    for b in range(BLOCKS):
        y, x = b // 4, b % 4
        first.append(block_at(y, x + 1))
        second.append(block_at(y + 1, x + 3))
        cycle = {(0, 0): (0, 2), (0, 1): (1, 2), (1, 1): (1, 0), (1, 0): (0, 0)}
        ny, nx = cycle[(y, x // 2)]
        third.append(block_at(ny, nx + x % 2))
        fourth.append(block_at(y + 1, x + 2))
    return [first, second, third, fourth]


PARTNERS = partner_tables()


def params():
    return pltpu.CompilerParams(vmem_limit_bytes=24 << 20)


def in_vmem(n):
    return [pl.BlockSpec(memory_space=pltpu.VMEM)] * n


def branch_sums(ref, lane):
    def add(k8, total):
        at = pl.ds(pl.multiple_of(k8 * 8, 8), 8)
        return total + ref[at, lane : lane + 128]

    total = lax.fori_loop(0, KS // 8, add, jnp.zeros((8, 128), F32), unroll=8)
    return jnp.sum(total, axis=0, keepdims=True)


def weigh_kernel(counts_hbm, totals_hbm, lengths_hbm, wt_ref, split_ref, col_ref, *scratch):
    counts_ref, totals_ref, lengths_ref, sems = scratch
    loads = [
        pltpu.make_async_copy(src, dst, sems.at[n])
        for n, (src, dst) in enumerate(
            ((counts_hbm, counts_ref), (totals_hbm, totals_ref), (lengths_hbm, lengths_ref))
        )
    ]
    for load in loads:
        load.start()
    for load in loads:
        load.wait()
    scaled = lengths_ref[...].astype(F32) * 0.001
    wt = (scaled * counts_ref[...].astype(F32)).T / totals_ref[...].astype(F32)
    wt_ref[...] = wt
    for n in range(8):
        x = wt[:, n * 32 : (n + 1) * 32]
        high = x.astype(BF16)
        rest = x - high.astype(F32)
        middle = rest.astype(BF16)
        low = (rest - middle.astype(F32)).astype(BF16)
        split_ref[n] = jnp.concatenate([high, middle, low, jnp.zeros_like(low)], axis=1)
    for h in range(2):
        sums = branch_sums(wt_ref, h * 128)
        col_ref[h * 128 : (h + 1) * 128, :] = jnp.broadcast_to(sums, (128, 128)).T


def weigh(counts, totals, lengths):
    return pl.pallas_call(
        weigh_kernel,
        out_shape=(
            jax.ShapeDtypeStruct((KS, ROWS), F32),
            jax.ShapeDtypeStruct((8, KS, 128), BF16),
            jax.ShapeDtypeStruct((ROWS, 128), F32),
        ),
        in_specs=[pl.BlockSpec(memory_space=pltpu.HBM)] * 3,
        out_specs=tuple(in_vmem(3)),
        scratch_shapes=[
            pltpu.VMEM((ROWS, KS), jnp.int32),
            pltpu.VMEM((1, ROWS), jnp.int32),
            pltpu.VMEM((1, KS), jnp.int32),
            pltpu.SemaphoreType.DMA((3,)),
        ],
        compiler_params=params(),
        name="weigh",
    )(counts, totals.reshape(1, ROWS), lengths.reshape(1, KS))


def spread_call(name, n_blocks, columns, width, group, mass_row, side=None):
    pairs = group // 2
    halves = 2 if side is None else 1
    groups = halves * ROWS // 2 // group

    def kernel(split_ref, col_ref, *refs):
        blocks = refs[:n_blocks]
        out_ref, pick_ref, even_ref, odd_ref = refs[n_blocks:]
        core = lax.axis_index("branch") % 2
        y = lax.axis_index("blk") // 4
        if side is None:
            base = 0
        else:
            base = (core if side == 0 else 1 - core) * groups

        part = lax.broadcasted_iota(jnp.int32, (128, 256), 0)
        lane = lax.broadcasted_iota(jnp.int32, (128, 256), 1)
        want = jnp.where(part < 96, part % 32 - lane // 128, -1)
        for p in range(16):
            pick_ref[p] = jnp.where(want == 2 * p, 1.0, 0.0).astype(BF16)

        def broadcast_pair(into, g, q, at=slice(0, KS)):
            pair = g * pairs + q
            into[q, at] = jnp.dot(
                split_ref[pair // 16, at], pick_ref[pair % 16], preferred_element_type=F32
            )

        def span(n, lane, at):
            if isinstance(lane, int):
                return blocks[n][at, lane : lane + 128]
            return blocks[n][at, pl.ds(pl.multiple_of(lane, 128), 128)]

        def columns_at(h):
            return columns(h if side is None else base // groups, y)

        for h in range(halves):
            below = [jnp.zeros((1, 128), F32)] * mass_row
            for n, lane in columns_at(h):
                total = jnp.zeros((8, 128), F32)
                for k8 in range(KS // 8):
                    total = total + span(n, lane, slice(k8 * 8, k8 * 8 + 8))
                below.append(jnp.sum(total, axis=0, keepdims=True))
            below += [jnp.zeros((1, 128), F32)] * (8 - len(below))
            out_ref[h, 128:136, 0:128] = jnp.concatenate(below, axis=0)

        for q in range(pairs):
            broadcast_pair(even_ref, base, q)

        def one_group(g, now, later):
            h = g * group // 128
            cols = columns_at(h)
            n_cols = len(cols)
            following = base + jnp.minimum(g + 1, groups - 1)
            steps = []
            if group == 8:
                for q in range(pairs):
                    broadcast_pair(later, following, q)
            else:
                steps = [(q, slice(k, k + 128)) for k in range(0, KS, 128) for q in range(pairs)]
            acc = [jnp.zeros((8, 128), F32)] * (group * n_cols)
            for k8 in range(KS // 8):
                if steps and k8 % 2 == 0:
                    q, at = steps[k8 // 2]
                    broadcast_pair(later, following, q, at)
                at = slice(k8 * 8, k8 * 8 + 8)
                spans = [span(n, lane, at) for n, lane in cols]
                for r in range(group):
                    own = now[r // 2, at, 128 * (r % 2) : 128 * (r % 2) + 128]
                    for j in range(n_cols):
                        acc[r * n_cols + j] += jnp.minimum(own, spans[j])
            for r0 in range(0, group, 8):
                row = pl.multiple_of(g * group + r0 - h * 128, 8)
                first = pl.multiple_of((base + g) * group + r0, 8)
                own_mass = col_ref[pl.ds(first, 8), :]
                for j in range(n_cols):
                    mass = out_ref[h, 128 + mass_row + j : 129 + mass_row + j, 0:128]
                    least = jnp.concatenate(
                        [
                            jnp.sum(acc[(r0 + r) * n_cols + j], axis=0, keepdims=True)
                            for r in range(8)
                        ],
                        axis=0,
                    )
                    out_ref[h, pl.ds(row, 8), 128 * j : 128 * j + 128] = (
                        own_mass + mass - 2.0 * least
                    )

        def two_groups(t, carry):
            one_group(2 * t, even_ref, odd_ref)
            one_group(2 * t + 1, odd_ref, even_ref)
            return carry

        lax.fori_loop(0, groups // 2, two_groups, 0)

    def call(split, col, *blocks):
        return pl.pallas_call(
            kernel,
            out_shape=jax.ShapeDtypeStruct((halves, 136, width), F32),
            in_specs=in_vmem(2 + n_blocks),
            out_specs=in_vmem(1)[0],
            scratch_shapes=[
                pltpu.VMEM((16, 128, 256), BF16),
                pltpu.VMEM((pairs, KS, 256), F32),
                pltpu.VMEM((pairs, KS, 256), F32),
            ],
            compiler_params=params(),
            cost_estimate=pl.CostEstimate(
                flops=halves * width * 128 * KS * 250, bytes_accessed=4 << 20, transcendentals=0
            ),
            name=name,
        )(split, col, *blocks)

    return call


def diagonal_columns(half, y):
    return [(0, 0), (0, 128)]


def first_columns(half, y):
    return [(0, 0), (0, 128), (1, 0), (1, 128)]


def second_columns(half, y):
    return [(0, 0), (0, 128), (1, (half ^ y) * 128)]


DIRECT = 1152


FIRST = 768
SECOND = 384
DIRECT = FIRST + SECOND


def pack_kernel(*refs):
    out_ref = refs[-1]
    core = lax.axis_index("branch") % 2
    lane = 0
    masses = jnp.zeros((8, 128), F32)
    for own, got in zip(refs[:-1:2], refs[1:-1:2], strict=True):
        half = core if own.shape[0] == 2 else 0
        width = own.shape[2]
        both = own[half, 0:128, :] + got[half, 0:128, :]
        out_ref[:, :, lane : lane + width] = both.reshape(16, 8, width)
        masses = masses + own[half, 128:136, 0:128] + got[half, 128:136, 0:128]
        lane += width
    out_ref[:, :, lane:] = jnp.broadcast_to(masses[None], (16, 8, 128))


def pack(*parts):
    width = sum(p.shape[2] for p in parts[::2]) + 128
    return pl.pallas_call(
        pack_kernel,
        out_shape=jax.ShapeDtypeStruct((16, 8, width), F32),
        in_specs=in_vmem(len(parts)),
        out_specs=in_vmem(1)[0],
        compiler_params=params(),
        name="pack",
    )(*parts)


def block_partner(b, slot):
    y, x = b // 4, b % 4
    if slot == 0:
        return b
    if slot == 1:
        return y * 4 + (x + 1) % 4
    if slot == 2:
        return (1 - y) * 4 + (x + 3) % 4
    if slot == 4:
        return (1 - y) * 4 + (x + 2) % 4
    if slot == 5:
        return y * 4 + (x + 3) % 4
    if slot == 6:
        return (1 - y) * 4 + (x + 1) % 4
    far = x // 2
    keep_y = (far == y) if slot == 3 else (far != y)
    return jnp.where(keep_y, y * 4 + (x + 2) % 4, (1 - y) * 4 + x)


def normalise_kernel(first_ref, second_ref, dist_ref, swap_ref):
    branch = lax.axis_index("branch")
    b = lax.axis_index("blk")
    core, place = branch % 2, branch // 2
    first = jnp.sum(first_ref[...], axis=0)
    second = jnp.sum(second_ref[...], axis=0)
    rows = [first[r : r + 1, FIRST:] for r in range(6)]
    rows += [second[r : r + 1, SECOND:] for r in range(3)]
    total = jnp.concatenate([first[:, :FIRST], second[:, :SECOND]], axis=1)
    mine = jnp.broadcast_to(jnp.where(core == 0, rows[0], rows[1]), (8, 128))
    lane = lax.broadcasted_iota(jnp.int32, (8, 128), 1)
    row = lax.broadcasted_iota(jnp.int32, (8, 128), 0)
    own = jnp.sum(jnp.where(lane == place * 8 + row, mine, 0.0), axis=1, keepdims=True)
    for j in range(DIRECT // 128):
        at = slice(128 * j, 128 * j + 128)
        dist_ref[:, at] = total[:, at] / (own + rows[j])
    swap_ref[...] = jnp.zeros_like(swap_ref)
    for slot in range(1, 4):
        swap_ref[block_partner(b, slot)] = dist_ref[:, slot * ROWS : (slot + 1) * ROWS]
    swap_ref[block_partner(b, 4), :, 0:128] = dist_ref[:, 4 * ROWS : DIRECT]


def normalise(first, second):
    return pl.pallas_call(
        normalise_kernel,
        out_shape=(
            jax.ShapeDtypeStruct((8, DIRECT), F32),
            jax.ShapeDtypeStruct((BLOCKS, 8, ROWS), F32),
        ),
        in_specs=in_vmem(2),
        out_specs=tuple(in_vmem(2)),
        compiler_params=params(),
        name="normalise",
    )(first, second)


def spread_out_kernel(dist_ref, swapped_ref, out_ref):
    b = lax.axis_index("blk")
    pieces = [dist_ref[...]]
    pieces += [swapped_ref[block_partner(b, slot)] for slot in (5, 6, 7)]
    pieces.append(swapped_ref[block_partner(b, 4), :, 0:128])
    whole = jnp.concatenate(pieces, axis=1)
    out_ref[...] = jnp.broadcast_to(whole[None], out_ref.shape)


def spread_out(dist, swapped):
    return pl.pallas_call(
        spread_out_kernel,
        out_shape=jax.ShapeDtypeStruct((16, 8, BLOCKS * ROWS), F32),
        in_specs=in_vmem(2),
        out_specs=in_vmem(1)[0],
        compiler_params=params(),
        name="spread_out",
    )(dist, swapped)


def assemble_kernel(own, other, out_ref, turned_ref, sems):
    core = lax.axis_index("branch") % 2
    b = lax.axis_index("blk")
    y = b // 4
    stores = []

    def store(src, rows, cols):
        copy = pltpu.make_async_copy(src, out_ref.at[rows, cols], sems.at[len(stores)])
        copy.start()
        stores.append(copy)

    def rows_of(half):
        return pl.ds(pl.multiple_of(half * 128, 128), 128)

    def columns(slot, half=None):
        first = block_partner(b, slot) * ROWS
        if half is None:
            return pl.ds(pl.multiple_of(first, ROWS), ROWS)
        return pl.ds(pl.multiple_of(first + half * 128, 128), 128)

    both = ((0, core, own), (1, 1 - core, other))
    for _, half, ref in both:
        rows = rows_of(half)
        for slot, lane in ((0, 0), (1, 256), (2, 512), (3, 768)):
            store(ref.at[:, lane : lane + ROWS], rows, columns(slot))
        store(ref.at[:, 1024:1152], rows, columns(4, half ^ y))
    for side, half, ref in both:
        for n, slot in enumerate((5, 6, 7)):
            lane = 1152 + n * ROWS
            turned_ref[side, n] = ref[:, lane : lane + ROWS].T
            store(turned_ref.at[side, n], slice(0, ROWS), columns(slot, half))
        turned_ref[side, 3, 0:128] = ref[:, 1920:2048].T
        store(turned_ref.at[side, 3, 0:128], rows_of(half ^ (1 - y)), columns(4, half))
    for copy in stores:
        copy.wait()


def assemble(*pieces):
    return pl.pallas_call(
        assemble_kernel,
        out_shape=jax.ShapeDtypeStruct((ROWS, BLOCKS * ROWS), F32),
        in_specs=in_vmem(2),
        out_specs=pl.BlockSpec(memory_space=pl.ANY),
        scratch_shapes=[
            pltpu.VMEM((2, 4, ROWS, 128), F32),
            pltpu.SemaphoreType.DMA((18,)),
        ],
        compiler_params=params(),
        name="assemble",
    )(*[p.reshape(128, p.shape[2]) for p in pieces])


def on_device(counts, totals, lengths):
    def from_partner(v, n):
        return lax.ppermute(v, "blk", [(PARTNERS[n][b], b) for b in range(BLOCKS)])

    def other_core(v):
        return lax.ppermute(v, "branch", [(i, i ^ 1) for i in range(32)])

    chips = [[2 * p + c for p in range(16)] for c in range(2)]

    def over_chips(v):
        return lax.all_to_all(v, "branch", 0, 0, axis_index_groups=chips)

    wt, split, mass_col = weigh(counts, totals, lengths)
    got = [from_partner(wt, n) for n in range(2)]
    diagonal = spread_call("diagonal", 1, diagonal_columns, 256, 16, 0)
    first = [spread_call(f"first{s}", 2, first_columns, 512, 8, 2, s) for s in range(2)]
    second = [spread_call(f"second{s}", 2, second_columns, 384, 8, 0, s) for s in range(2)]

    def after(v, *others):
        return lax.optimization_barrier((v, *others))[0]

    part0 = diagonal(split, mass_col, wt)
    later = after(wt, part0)
    got += [from_partner(later, n) for n in (2, 3)]
    received0 = other_core(part0)
    sent1 = first[1](split, mass_col, *got[:2])
    received1 = other_core(sent1)
    part1 = first[0](split, mass_col, after(got[0], sent1), got[1])
    payload1 = pack(part0, received0, part1, received1)
    shards1 = over_chips(payload1)

    third = after(got[2], payload1)
    sent2 = second[1](split, mass_col, third, got[3])
    received2 = other_core(sent2)
    part2 = second[0](split, mass_col, after(third, sent2), got[3])
    shards2 = over_chips(pack(part2, received2))

    dist, swap = normalise(shards1, shards2)
    whole = over_chips(spread_out(dist, lax.all_to_all(swap, "blk", 0, 0)))
    return assemble(whole, other_core(whole))


def solution(mesh):
    placed = (P("blk", "branch"), P("blk"), P("branch"))
    return jax.shard_map(
        on_device, mesh=mesh, in_specs=placed, out_specs=P("blk", None), check_vma=False
    )
```

```python
import jax
import jax.numpy as jnp
from jax import lax
from jax.experimental import pallas as pl
from jax.experimental.pallas import tpu as pltpu
from jax.sharding import PartitionSpec as P

F32 = jnp.float32
BF16 = jnp.bfloat16
ROWS = 256
KS = 512
BLOCKS = 8
GROUP = 8
PAIRS = GROUP // 2
GROUPS = ROWS // GROUP


def block_at(y, x):
    return (y % 2) * 4 + x % 4


def partner_tables():
    first, second, third, fourth = [], [], [], []
    for b in range(BLOCKS):
        y, x = b // 4, b % 4
        first.append(block_at(y, x + 1))
        second.append(block_at(y + 1, x + 3))
        cycle = {(0, 0): (0, 2), (0, 1): (1, 2), (1, 1): (1, 0), (1, 0): (0, 0)}
        ny, nx = cycle[(y, x // 2)]
        third.append(block_at(ny, nx + x % 2))
        fourth.append(block_at(y + 1, x + 2))
    return [first, second, third, fourth]


PARTNERS = partner_tables()


def params():
    return pltpu.CompilerParams(vmem_limit_bytes=24 << 20)


def in_vmem(n):
    return [pl.BlockSpec(memory_space=pltpu.VMEM)] * n


def branch_sums(ref, lane):
    def add(k8, total):
        at = pl.ds(pl.multiple_of(k8 * 8, 8), 8)
        return total + ref[at, lane : lane + 128]

    total = lax.fori_loop(0, KS // 8, add, jnp.zeros((8, 128), F32), unroll=8)
    return jnp.sum(total, axis=0, keepdims=True)


def weigh_kernel(counts_hbm, totals_hbm, lengths_hbm, wt_ref, split_ref, col_ref, *scratch):
    counts_ref, totals_ref, lengths_ref, sems = scratch
    loads = [
        pltpu.make_async_copy(src, dst, sems.at[n])
        for n, (src, dst) in enumerate(
            ((counts_hbm, counts_ref), (totals_hbm, totals_ref), (lengths_hbm, lengths_ref))
        )
    ]
    for load in loads:
        load.start()
    for load in loads:
        load.wait()
    scaled = lengths_ref[...].astype(F32) * 0.001
    wt = (scaled * counts_ref[...].astype(F32)).T / totals_ref[...].astype(F32)
    wt_ref[...] = wt
    for n in range(8):
        x = wt[:, n * 32 : (n + 1) * 32]
        high = x.astype(BF16)
        rest = x - high.astype(F32)
        middle = rest.astype(BF16)
        low = (rest - middle.astype(F32)).astype(BF16)
        split_ref[n] = jnp.concatenate([high, middle, low, jnp.zeros_like(low)], axis=1)
    for h in range(2):
        sums = branch_sums(wt_ref, h * 128)
        col_ref[h * 128 : (h + 1) * 128, :] = jnp.broadcast_to(sums, (128, 128)).T


def weigh(counts, totals, lengths):
    return pl.pallas_call(
        weigh_kernel,
        out_shape=(
            jax.ShapeDtypeStruct((KS, ROWS), F32),
            jax.ShapeDtypeStruct((8, KS, 128), BF16),
            jax.ShapeDtypeStruct((ROWS, 128), F32),
        ),
        in_specs=[pl.BlockSpec(memory_space=pltpu.HBM)] * 3,
        out_specs=tuple(in_vmem(3)),
        scratch_shapes=[
            pltpu.VMEM((ROWS, KS), jnp.int32),
            pltpu.VMEM((1, ROWS), jnp.int32),
            pltpu.VMEM((1, KS), jnp.int32),
            pltpu.SemaphoreType.DMA((3,)),
        ],
        compiler_params=params(),
        name="weigh",
    )(counts, totals.reshape(1, ROWS), lengths.reshape(1, KS))


def spread_call(name, n_blocks, columns, width, group, mass_row, side=None):
    pairs = group // 2
    halves = 2 if side is None else 1
    groups = halves * ROWS // 2 // group

    def kernel(split_ref, col_ref, *refs):
        blocks = refs[:n_blocks]
        out_ref, pick_ref, even_ref, odd_ref = refs[n_blocks:]
        core = lax.axis_index("branch") % 2
        y = lax.axis_index("blk") // 4
        if side is None:
            base = 0
        else:
            base = (core if side == 0 else 1 - core) * groups

        part = lax.broadcasted_iota(jnp.int32, (128, 256), 0)
        lane = lax.broadcasted_iota(jnp.int32, (128, 256), 1)
        want = jnp.where(part < 96, part % 32 - lane // 128, -1)
        for p in range(16):
            pick_ref[p] = jnp.where(want == 2 * p, 1.0, 0.0).astype(BF16)

        def broadcast_pair(into, g, q, at=slice(0, KS)):
            pair = g * pairs + q
            into[q, at] = jnp.dot(
                split_ref[pair // 16, at], pick_ref[pair % 16], preferred_element_type=F32
            )

        def span(n, lane, at):
            if isinstance(lane, int):
                return blocks[n][at, lane : lane + 128]
            return blocks[n][at, pl.ds(pl.multiple_of(lane, 128), 128)]

        def columns_at(h):
            return columns(h if side is None else base // groups, y)

        for h in range(halves):
            below = [jnp.zeros((1, 128), F32)] * mass_row
            for n, lane in columns_at(h):
                total = jnp.zeros((8, 128), F32)
                for k8 in range(KS // 8):
                    total = total + span(n, lane, slice(k8 * 8, k8 * 8 + 8))
                below.append(jnp.sum(total, axis=0, keepdims=True))
            below += [jnp.zeros((1, 128), F32)] * (8 - len(below))
            out_ref[h, 128:136, 0:128] = jnp.concatenate(below, axis=0)

        for q in range(pairs):
            broadcast_pair(even_ref, base, q)

        def one_group(g, now, later):
            h = g * group // 128
            cols = columns_at(h)
            n_cols = len(cols)
            following = base + jnp.minimum(g + 1, groups - 1)
            steps = []
            if group == 8:
                for q in range(pairs):
                    broadcast_pair(later, following, q)
            else:
                steps = [(q, slice(k, k + 128)) for k in range(0, KS, 128) for q in range(pairs)]
            acc = [jnp.zeros((8, 128), F32)] * (group * n_cols)
            for k8 in range(KS // 8):
                if steps and k8 % 2 == 0:
                    q, at = steps[k8 // 2]
                    broadcast_pair(later, following, q, at)
                at = slice(k8 * 8, k8 * 8 + 8)
                spans = [span(n, lane, at) for n, lane in cols]
                for r in range(group):
                    own = now[r // 2, at, 128 * (r % 2) : 128 * (r % 2) + 128]
                    for j in range(n_cols):
                        acc[r * n_cols + j] += jnp.minimum(own, spans[j])
            for r0 in range(0, group, 8):
                row = pl.multiple_of(g * group + r0 - h * 128, 8)
                first = pl.multiple_of((base + g) * group + r0, 8)
                own_mass = col_ref[pl.ds(first, 8), :]
                for j in range(n_cols):
                    mass = out_ref[h, 128 + mass_row + j : 129 + mass_row + j, 0:128]
                    least = jnp.concatenate(
                        [
                            jnp.sum(acc[(r0 + r) * n_cols + j], axis=0, keepdims=True)
                            for r in range(8)
                        ],
                        axis=0,
                    )
                    out_ref[h, pl.ds(row, 8), 128 * j : 128 * j + 128] = (
                        own_mass + mass - 2.0 * least
                    )

        def two_groups(t, carry):
            one_group(2 * t, even_ref, odd_ref)
            one_group(2 * t + 1, odd_ref, even_ref)
            return carry

        lax.fori_loop(0, groups // 2, two_groups, 0)

    def call(split, col, *blocks):
        return pl.pallas_call(
            kernel,
            out_shape=jax.ShapeDtypeStruct((halves, 136, width), F32),
            in_specs=in_vmem(2 + n_blocks),
            out_specs=in_vmem(1)[0],
            scratch_shapes=[
                pltpu.VMEM((16, 128, 256), BF16),
                pltpu.VMEM((pairs, KS, 256), F32),
                pltpu.VMEM((pairs, KS, 256), F32),
            ],
            compiler_params=params(),
            cost_estimate=pl.CostEstimate(
                flops=halves * width * 128 * KS * 250, bytes_accessed=4 << 20, transcendentals=0
            ),
            name=name,
        )(split, col, *blocks)

    return call


def diagonal_columns(half, y):
    return [(0, 0), (0, 128)]


def first_columns(half, y):
    return [(0, 0), (0, 128), (1, 0), (1, 128)]


def second_columns(half, y):
    return [(0, 0), (0, 128), (1, (half ^ y) * 128)]


DIRECT = 1152


def pack_kernel(own0, got0, own1, got1, own2, got2, out_ref):
    core = lax.axis_index("branch") % 2
    lane = 0
    masses = []
    for own, got in ((own0, got0), (own1, got1), (own2, got2)):
        half = core if own.shape[0] == 2 else 0
        width = own.shape[2]
        both = own[half, 0:128, :] + got[half, 0:128, :]
        out_ref[:, :, lane : lane + width] = both.reshape(16, 8, width)
        masses.append(own[half, 128:136, 0:128] + got[half, 128:136, 0:128])
        lane += width
    for block in (masses[0] + masses[1], masses[2]):
        out_ref[:, :, lane : lane + 128] = jnp.broadcast_to(block[None], (16, 8, 128))
        lane += 128


def pack(*parts):
    return pl.pallas_call(
        pack_kernel,
        out_shape=jax.ShapeDtypeStruct((16, 8, DIRECT + 256), F32),
        in_specs=in_vmem(6),
        out_specs=in_vmem(1)[0],
        compiler_params=params(),
        name="pack",
    )(*parts)


def block_partner(b, slot):
    y, x = b // 4, b % 4
    if slot == 0:
        return b
    if slot == 1:
        return y * 4 + (x + 1) % 4
    if slot == 2:
        return (1 - y) * 4 + (x + 3) % 4
    if slot == 4:
        return (1 - y) * 4 + (x + 2) % 4
    if slot == 5:
        return y * 4 + (x + 3) % 4
    if slot == 6:
        return (1 - y) * 4 + (x + 1) % 4
    far = x // 2
    keep_y = (far == y) if slot == 3 else (far != y)
    return jnp.where(keep_y, y * 4 + (x + 2) % 4, (1 - y) * 4 + x)


def normalise_kernel(shards_ref, out_ref):
    branch = lax.axis_index("branch")
    core, place = branch % 2, branch // 2
    total = jnp.sum(shards_ref[...], axis=0)
    rows = [total[r : r + 1, DIRECT : DIRECT + 128] for r in range(6)]
    rows += [total[r : r + 1, DIRECT + 128 : DIRECT + 256] for r in range(3)]
    mine = jnp.broadcast_to(jnp.where(core == 0, rows[0], rows[1]), (8, 128))
    lane = lax.broadcasted_iota(jnp.int32, (8, 128), 1)
    row = lax.broadcasted_iota(jnp.int32, (8, 128), 0)
    own = jnp.sum(jnp.where(lane == place * 8 + row, mine, 0.0), axis=1, keepdims=True)
    for j in range(DIRECT // 128):
        at = slice(128 * j, 128 * j + 128)
        dist = total[:, at] / (own + rows[j])
        out_ref[:, :, at] = jnp.broadcast_to(dist[None], (16, 8, 128))


def normalise(shards):
    return pl.pallas_call(
        normalise_kernel,
        out_shape=jax.ShapeDtypeStruct((16, 8, DIRECT), F32),
        in_specs=in_vmem(1),
        out_specs=in_vmem(1)[0],
        compiler_params=params(),
        name="normalise",
    )(shards)


def assemble_kernel(own, other, own_swapped, other_swapped, out_ref, turned_ref, sems):
    core = lax.axis_index("branch") % 2
    b = lax.axis_index("blk")
    y = b // 4
    stores = []

    def store(src, rows, cols):
        copy = pltpu.make_async_copy(src, out_ref.at[rows, cols], sems.at[len(stores)])
        copy.start()
        stores.append(copy)

    def rows_of(half):
        return pl.ds(pl.multiple_of(half * 128, 128), 128)

    def columns(slot, half=None):
        first = block_partner(b, slot) * ROWS
        if half is None:
            return pl.ds(pl.multiple_of(first, ROWS), ROWS)
        return pl.ds(pl.multiple_of(first + half * 128, 128), 128)

    for half, ref in ((core, own), (1 - core, other)):
        rows = rows_of(half)
        for slot in range(4):
            store(ref.at[:, slot * ROWS : (slot + 1) * ROWS], rows, columns(slot))
        store(ref.at[:, 4 * ROWS : DIRECT], rows, columns(4, half ^ y))
    for side, half, ref in ((0, core, own_swapped), (1, 1 - core, other_swapped)):
        for n, slot in enumerate((5, 6, 7)):
            turned_ref[side, n] = ref[:, n * ROWS : (n + 1) * ROWS].T
            store(turned_ref.at[side, n], slice(0, ROWS), columns(slot, half))
        turned_ref[side, 3, 0:128] = ref[:, 3 * ROWS :].T
        store(turned_ref.at[side, 3, 0:128], rows_of(half ^ (1 - y)), columns(4, half))
    for copy in stores:
        copy.wait()


def assemble(*pieces):
    return pl.pallas_call(
        assemble_kernel,
        out_shape=jax.ShapeDtypeStruct((ROWS, BLOCKS * ROWS), F32),
        in_specs=in_vmem(4),
        out_specs=pl.BlockSpec(memory_space=pl.ANY),
        scratch_shapes=[
            pltpu.VMEM((2, 4, ROWS, 128), F32),
            pltpu.SemaphoreType.DMA((18,)),
        ],
        compiler_params=params(),
        name="assemble",
    )(*pieces)


def on_device(counts, totals, lengths):
    def from_partner(v, n):
        return lax.ppermute(v, "blk", [(PARTNERS[n][b], b) for b in range(BLOCKS)])

    def other_core(v):
        return lax.ppermute(v, "branch", [(i, i ^ 1) for i in range(32)])

    chips = [[2 * p + c for p in range(16)] for c in range(2)]

    def over_chips(v):
        return lax.all_to_all(v, "branch", 0, 0, axis_index_groups=chips)

    wt, split, mass_col = weigh(counts, totals, lengths)
    got = [from_partner(wt, n) for n in range(2)]
    diagonal = spread_call("diagonal", 1, diagonal_columns, 256, 16, 0)
    first = spread_call("first", 2, first_columns, 512, 8, 2)
    second = [spread_call(f"second{s}", 2, second_columns, 384, 8, 0, s) for s in range(2)]

    part0 = diagonal(split, mass_col, wt)
    later = lax.optimization_barrier((wt, part0))[0]
    got += [from_partner(later, n) for n in (2, 3)]
    received0 = other_core(part0)
    part1 = first(split, mass_col, got[0], got[1])
    received1 = other_core(part1)
    third = lax.optimization_barrier((got[2], part1))[0]
    sent2 = second[1](split, mass_col, third, got[3])
    received2 = other_core(sent2)
    third = lax.optimization_barrier((third, sent2))[0]
    part2 = second[0](split, mass_col, third, got[3])

    shards = over_chips(pack(part0, received0, part1, received1, part2, received2))
    own = over_chips(normalise(shards)).reshape(128, DIRECT)
    swapped = []
    for n in range(4):
        tile = own[:, (n + 1) * ROWS : min((n + 2) * ROWS, DIRECT)]
        swapped.append(lax.ppermute(tile, "blk", [(b, PARTNERS[n][b]) for b in range(BLOCKS)]))
    other = other_core(own)
    swapped = jnp.concatenate(swapped, axis=1)
    return assemble(own, other, swapped, other_core(swapped))


def solution(mesh):
    placed = (P("blk", "branch"), P("blk"), P("branch"))
    return jax.shard_map(
        on_device, mesh=mesh, in_specs=placed, out_specs=P("blk", None), check_vma=False
    )
```

```python
import jax
import jax.numpy as jnp
from jax import lax
from jax.experimental import pallas as pl
from jax.experimental.pallas import tpu as pltpu
from jax.sharding import PartitionSpec as P

F32 = jnp.float32
BF16 = jnp.bfloat16
ROWS = 256
KS = 512
BLOCKS = 8
GROUP = 8
PAIRS = GROUP // 2
GROUPS = ROWS // GROUP


def block_at(y, x):
    return (y % 2) * 4 + x % 4


def partner_tables():
    first, second, third, fourth = [], [], [], []
    for b in range(BLOCKS):
        y, x = b // 4, b % 4
        first.append(block_at(y, x + 1))
        second.append(block_at(y + 1, x + 3))
        cycle = {(0, 0): (0, 2), (0, 1): (1, 2), (1, 1): (1, 0), (1, 0): (0, 0)}
        ny, nx = cycle[(y, x // 2)]
        third.append(block_at(ny, nx + x % 2))
        fourth.append(block_at(y + 1, x + 2))
    return [first, second, third, fourth]


PARTNERS = partner_tables()


def params():
    return pltpu.CompilerParams(vmem_limit_bytes=24 << 20)


def in_vmem(n):
    return [pl.BlockSpec(memory_space=pltpu.VMEM)] * n


def row_sums(parts):
    parts = parts + [jnp.zeros((8, 128), F32)] * (8 - len(parts))
    sub = lax.broadcasted_iota(jnp.int32, (8, 128), 0)
    for bit in (4, 2, 1):
        first = (sub & bit) == 0
        merged = []
        for r in range(bit):
            kept = jnp.where(first, parts[r], parts[r + bit])
            other = jnp.where(first, parts[r + bit], parts[r])
            if bit == 4:
                moved = pltpu.roll(other, 4, 0)
            else:
                moved = jnp.where(first, pltpu.roll(other, 8 - bit, 0), pltpu.roll(other, bit, 0))
            merged.append(kept + moved)
        parts = merged
    return parts[0]


def branch_sums(read):
    total = jnp.zeros((8, 128), F32)
    for k8 in range(KS // 8):
        total = total + read(slice(k8 * 8, k8 * 8 + 8))
    return total


def weigh_kernel(counts_hbm, totals_hbm, lengths_hbm, wt_ref, split_ref, col_ref, *scratch):
    counts_ref, totals_ref, lengths_ref, sems = scratch
    loads = [
        pltpu.make_async_copy(src, dst, sems.at[n])
        for n, (src, dst) in enumerate(
            ((counts_hbm, counts_ref), (totals_hbm, totals_ref), (lengths_hbm, lengths_ref))
        )
    ]
    for load in loads:
        load.start()
    for load in loads:
        load.wait()
    scaled = lengths_ref[...].astype(F32) * 0.001
    wt = (scaled * counts_ref[...].astype(F32)).T / totals_ref[...].astype(F32)
    wt_ref[...] = wt
    for n in range(8):
        x = wt[:, n * 32 : (n + 1) * 32]
        high = x.astype(BF16)
        rest = x - high.astype(F32)
        middle = rest.astype(BF16)
        low = (rest - middle.astype(F32)).astype(BF16)
        split_ref[n] = jnp.concatenate([high, middle, low, jnp.zeros_like(low)], axis=1)
    sums = row_sums(
        [branch_sums(lambda at, h=h: wt_ref[at, h * 128 : h * 128 + 128]) for h in range(2)]
    )
    for h in range(2):
        col_ref[h * 128 : (h + 1) * 128, :] = jnp.broadcast_to(sums[h : h + 1], (128, 128)).T


def weigh(counts, totals, lengths):
    return pl.pallas_call(
        weigh_kernel,
        out_shape=(
            jax.ShapeDtypeStruct((KS, ROWS), F32),
            jax.ShapeDtypeStruct((8, KS, 128), BF16),
            jax.ShapeDtypeStruct((ROWS, 128), F32),
        ),
        in_specs=[pl.BlockSpec(memory_space=pltpu.HBM)] * 3,
        out_specs=tuple(in_vmem(3)),
        scratch_shapes=[
            pltpu.VMEM((ROWS, KS), jnp.int32),
            pltpu.VMEM((1, ROWS), jnp.int32),
            pltpu.VMEM((1, KS), jnp.int32),
            pltpu.SemaphoreType.DMA((3,)),
        ],
        compiler_params=params(),
        name="weigh",
    )(counts, totals.reshape(1, ROWS), lengths.reshape(1, KS))


def spread_call(name, n_blocks, columns, width, group, mass_row, half=None, side=None):
    pairs = group // 2
    groups = ROWS // 2 // group

    def kernel(split_ref, col_ref, *refs):
        blocks = refs[:n_blocks]
        out_ref, pick_ref, even_ref, odd_ref = refs[n_blocks:]
        core = lax.axis_index("branch") % 2
        y = lax.axis_index("blk") // 4
        if side is None:
            rows_half = half
        else:
            rows_half = core if side == 0 else 1 - core
        base = rows_half * groups
        cols = columns(rows_half, y)
        n_cols = len(cols)

        part = lax.broadcasted_iota(jnp.int32, (128, 256), 0)
        lane = lax.broadcasted_iota(jnp.int32, (128, 256), 1)
        want = jnp.where(part < 96, part % 32 - lane // 128, -1)
        for p in range(16):
            pick_ref[p] = jnp.where(want == 2 * p, 1.0, 0.0).astype(BF16)

        def broadcast_pair(into, g, q, at=slice(0, KS)):
            pair = g * pairs + q
            into[q, at] = jnp.dot(
                split_ref[pair // 16, at], pick_ref[pair % 16], preferred_element_type=F32
            )

        def span(n, lane, at):
            if isinstance(lane, int):
                return blocks[n][at, lane : lane + 128]
            return blocks[n][at, pl.ds(pl.multiple_of(lane, 128), 128)]

        totals = [
            branch_sums(lambda at, n=n, lane=lane: span(n, lane, at)) for n, lane in cols
        ]
        masses = row_sums([jnp.zeros((8, 128), F32)] * mass_row + totals)
        out_ref[128:136, 0:128] = masses

        for q in range(pairs):
            broadcast_pair(even_ref, base, q)

        def one_group(g, now, later):
            following = base + jnp.minimum(g + 1, groups - 1)
            steps = []
            if group == 8:
                for q in range(pairs):
                    broadcast_pair(later, following, q)
            else:
                steps = [(q, slice(k, k + 128)) for k in range(0, KS, 128) for q in range(pairs)]
            acc = [jnp.zeros((8, 128), F32)] * (group * n_cols)
            for k8 in range(KS // 8):
                if steps and k8 % 2 == 0:
                    q, at = steps[k8 // 2]
                    broadcast_pair(later, following, q, at)
                at = slice(k8 * 8, k8 * 8 + 8)
                spans = [span(n, lane, at) for n, lane in cols]
                for r in range(group):
                    own = now[r // 2, at, 128 * (r % 2) : 128 * (r % 2) + 128]
                    for j in range(n_cols):
                        acc[r * n_cols + j] += jnp.minimum(own, spans[j])
            for r0 in range(0, group, 8):
                row = pl.multiple_of(g * group + r0, 8)
                first = pl.multiple_of((base + g) * group + r0, 8)
                own_mass = col_ref[pl.ds(first, 8), :]
                for j in range(n_cols):
                    mass = out_ref[128 + mass_row + j : 129 + mass_row + j, 0:128]
                    least = row_sums([acc[(r0 + r) * n_cols + j] for r in range(8)])
                    out_ref[pl.ds(row, 8), 128 * j : 128 * j + 128] = (
                        own_mass + mass - 2.0 * least
                    )

        def two_groups(t, carry):
            one_group(2 * t, even_ref, odd_ref)
            one_group(2 * t + 1, odd_ref, even_ref)
            return carry

        lax.fori_loop(0, groups // 2, two_groups, 0)

    def call(split, col, *blocks):
        return pl.pallas_call(
            kernel,
            out_shape=jax.ShapeDtypeStruct((136, width), F32),
            in_specs=in_vmem(2 + n_blocks),
            out_specs=in_vmem(1)[0],
            scratch_shapes=[
                pltpu.VMEM((16, 128, 256), BF16),
                pltpu.VMEM((pairs, KS, 256), F32),
                pltpu.VMEM((pairs, KS, 256), F32),
            ],
            compiler_params=params(),
            cost_estimate=pl.CostEstimate(
                flops=width * 128 * KS * 250, bytes_accessed=4 << 20, transcendentals=0
            ),
            name=name,
        )(split, col, *blocks)

    return call


def diagonal_columns(half, y):
    return [(0, 0), (0, 128)]


def first_columns(half, y):
    return [(0, 0), (0, 128), (1, 0), (1, 128)]


def lower_columns(half, y):
    return first_columns(half, y) + [(2, 128)]


def second_columns(half, y):
    return [(0, 0), (0, 128), (1, (half ^ y) * 128)]


DIRECT = 1152


def pack_kernel(*refs):
    diagonal, upper, lower, second = [
        (own, got) for own, got in zip(refs[:8:2], refs[1:8:2], strict=True)
    ]
    out_ref = refs[8]
    core = lax.axis_index("branch") % 2

    def both(parts, rows=slice(0, 128), lanes=slice(None)):
        return parts[0][rows, lanes] + parts[1][rows, lanes]

    def put(lane, value):
        out_ref[:, :, lane : lane + value.shape[1]] = value.reshape(16, 8, -1)

    def put_masses(lane, block):
        out_ref[:, :, lane : lane + 128] = jnp.broadcast_to(block[None], (16, 8, 128))

    below, masses = slice(128, 136), slice(0, 128)

    @pl.when(core == 0)
    def _():
        put(0, both(diagonal))
        put(256, both(upper))
        put_masses(DIRECT, both(diagonal, below, masses) + both(upper, below, masses))

    @pl.when(core == 1)
    def _():
        put(0, jnp.zeros((128, 128), F32))
        put(128, both(lower, lanes=slice(512, 640)))
        put(256, both(lower, lanes=slice(0, 512)))
        block = both(lower, below, masses)
        none = jnp.zeros((1, 128), F32)
        put_masses(DIRECT, jnp.concatenate([none, block[6:7], block[2:6], none, none]))

    put(768, both(second))
    put_masses(DIRECT + 128, both(second, below, masses))


def pack(*parts):
    return pl.pallas_call(
        pack_kernel,
        out_shape=jax.ShapeDtypeStruct((16, 8, DIRECT + 256), F32),
        in_specs=in_vmem(8),
        out_specs=in_vmem(1)[0],
        compiler_params=params(),
        name="pack",
    )(*parts)


def block_partner(b, slot):
    y, x = b // 4, b % 4
    if slot == 0:
        return b
    if slot == 1:
        return y * 4 + (x + 1) % 4
    if slot == 2:
        return (1 - y) * 4 + (x + 3) % 4
    if slot == 4:
        return (1 - y) * 4 + (x + 2) % 4
    if slot == 5:
        return y * 4 + (x + 3) % 4
    if slot == 6:
        return (1 - y) * 4 + (x + 1) % 4
    far = x // 2
    keep_y = (far == y) if slot == 3 else (far != y)
    return jnp.where(keep_y, y * 4 + (x + 2) % 4, (1 - y) * 4 + x)


def normalise_kernel(shards_ref, out_ref):
    branch = lax.axis_index("branch")
    core, place = branch % 2, branch // 2
    total = jnp.sum(shards_ref[...], axis=0)
    rows = [total[r : r + 1, DIRECT : DIRECT + 128] for r in range(6)]
    rows += [total[r : r + 1, DIRECT + 128 : DIRECT + 256] for r in range(3)]
    mine = jnp.broadcast_to(jnp.where(core == 0, rows[0], rows[1]), (8, 128))
    lane = lax.broadcasted_iota(jnp.int32, (8, 128), 1)
    row = lax.broadcasted_iota(jnp.int32, (8, 128), 0)
    own = jnp.sum(jnp.where(lane == place * 8 + row, mine, 0.0), axis=1, keepdims=True)
    for j in range(DIRECT // 128):
        at = slice(128 * j, 128 * j + 128)
        dist = total[:, at] / (own + rows[j])
        out_ref[:, :, at] = jnp.broadcast_to(dist[None], (16, 8, 128))


def normalise(shards):
    return pl.pallas_call(
        normalise_kernel,
        out_shape=jax.ShapeDtypeStruct((16, 8, DIRECT), F32),
        in_specs=in_vmem(1),
        out_specs=in_vmem(1)[0],
        compiler_params=params(),
        name="normalise",
    )(shards)


def assemble_kernel(own, other, own_swapped, other_swapped, out_ref, turned_ref, sems):
    core = lax.axis_index("branch") % 2
    b = lax.axis_index("blk")
    y = b // 4
    stores = []

    def store(src, rows, cols):
        copy = pltpu.make_async_copy(src, out_ref.at[rows, cols], sems.at[len(stores)])
        copy.start()
        stores.append(copy)

    def rows_of(half):
        return pl.ds(pl.multiple_of(half * 128, 128), 128)

    def columns(slot, half=None):
        first = block_partner(b, slot) * ROWS
        if half is None:
            return pl.ds(pl.multiple_of(first, ROWS), ROWS)
        return pl.ds(pl.multiple_of(first + half * 128, 128), 128)

    for half, ref in ((core, own), (1 - core, other)):
        rows = rows_of(half)
        store(ref.at[:, 128:256], rows, columns(0, 1))
        for slot in range(1, 4):
            store(ref.at[:, slot * ROWS : (slot + 1) * ROWS], rows, columns(slot))
        store(ref.at[:, 4 * ROWS : DIRECT], rows, columns(4, half ^ y))
    upper = jnp.where(core == 0, own[:, 0:256], other[:, 0:256])
    turned_ref[0, 3, 128:256] = upper[:, 0:128]
    turned_ref[1, 3, 128:256] = upper[:, 128:256].T
    for half in range(2):
        store(turned_ref.at[half, 3, 128:256], rows_of(half), columns(0, 0))
    for side, half, ref in ((0, core, own_swapped), (1, 1 - core, other_swapped)):
        for n, slot in enumerate((5, 6, 7)):
            turned_ref[side, n] = ref[:, n * ROWS : (n + 1) * ROWS].T
            store(turned_ref.at[side, n], slice(0, ROWS), columns(slot, half))
        turned_ref[side, 3, 0:128] = ref[:, 3 * ROWS :].T
        store(turned_ref.at[side, 3, 0:128], rows_of(half ^ (1 - y)), columns(4, half))
    for copy in stores:
        copy.wait()


def assemble(*pieces):
    return pl.pallas_call(
        assemble_kernel,
        out_shape=jax.ShapeDtypeStruct((ROWS, BLOCKS * ROWS), F32),
        in_specs=in_vmem(4),
        out_specs=pl.BlockSpec(memory_space=pl.ANY),
        scratch_shapes=[
            pltpu.VMEM((2, 4, ROWS, 128), F32),
            pltpu.SemaphoreType.DMA((20,)),
        ],
        compiler_params=params(),
        name="assemble",
    )(*pieces)


def on_device(counts, totals, lengths):
    def from_partner(v, n):
        return lax.ppermute(v, "blk", [(PARTNERS[n][b], b) for b in range(BLOCKS)])

    def other_core(v):
        return lax.ppermute(v, "branch", [(i, i ^ 1) for i in range(32)])

    chips = [[2 * p + c for p in range(16)] for c in range(2)]

    def over_chips(v):
        return lax.all_to_all(v, "branch", 0, 0, axis_index_groups=chips)

    wt, split, mass_col = weigh(counts, totals, lengths)
    got = [from_partner(wt, n) for n in range(2)]
    diagonal = spread_call("diagonal", 1, diagonal_columns, 256, 16, 0, half=0)
    upper = spread_call("upper", 2, first_columns, 512, 8, 2, half=0)
    lower = spread_call("lower", 3, lower_columns, 640, 8, 2, half=1)
    second = [spread_call(f"second{s}", 2, second_columns, 384, 8, 0, side=s) for s in range(2)]

    def after(v, *others):
        return lax.optimization_barrier((v, *others))[0]

    part0 = diagonal(split, mass_col, wt)
    later = after(wt, part0)
    got += [from_partner(later, n) for n in (2, 3)]
    part1 = upper(split, mass_col, *got[:2])
    part2 = lower(split, mass_col, after(got[0], part1), got[1], wt)
    third = after(got[2], part2)
    sent3 = second[1](split, mass_col, third, got[3])
    part3 = second[0](split, mass_col, after(third, sent3), got[3])

    parts = []
    for own, sent in ((part0, part0), (part1, part1), (part2, part2), (part3, sent3)):
        parts += [own, other_core(sent)]
    shards = over_chips(pack(*parts))
    own = over_chips(normalise(shards)).reshape(128, DIRECT)
    swapped = []
    for n in range(4):
        tile = own[:, (n + 1) * ROWS : min((n + 2) * ROWS, DIRECT)]
        swapped.append(lax.ppermute(tile, "blk", [(b, PARTNERS[n][b]) for b in range(BLOCKS)]))
    other = other_core(own)
    swapped = jnp.concatenate(swapped, axis=1)
    return assemble(own, other, swapped, other_core(swapped))


def solution(mesh):
    placed = (P("blk", "branch"), P("blk"), P("branch"))
    return jax.shard_map(
        on_device, mesh=mesh, in_specs=placed, out_specs=P("blk", None), check_vma=False
    )
```

```python
import jax
import jax.numpy as jnp
from jax import lax
from jax.experimental import pallas as pl
from jax.experimental.pallas import tpu as pltpu
from jax.sharding import PartitionSpec as P

F32 = jnp.float32
BF16 = jnp.bfloat16
ROWS = 256
KS = 512
BLOCKS = 8
GROUP = 8
PAIRS = GROUP // 2
GROUPS = ROWS // GROUP


def block_at(y, x):
    return (y % 2) * 4 + x % 4


def partner_tables():
    first, second, third, fourth = [], [], [], []
    for b in range(BLOCKS):
        y, x = b // 4, b % 4
        first.append(block_at(y, x + 1))
        second.append(block_at(y + 1, x + 3))
        cycle = {(0, 0): (0, 2), (0, 1): (1, 2), (1, 1): (1, 0), (1, 0): (0, 0)}
        ny, nx = cycle[(y, x // 2)]
        third.append(block_at(ny, nx + x % 2))
        fourth.append(block_at(y + 1, x + 2))
    return [first, second, third, fourth]


PARTNERS = partner_tables()


def params():
    return pltpu.CompilerParams(vmem_limit_bytes=24 << 20)


def in_vmem(n):
    return [pl.BlockSpec(memory_space=pltpu.VMEM)] * n


def row_sums(parts):
    parts = parts + [jnp.zeros((8, 128), F32)] * (8 - len(parts))
    sub = lax.broadcasted_iota(jnp.int32, (8, 128), 0)
    for bit in (4, 2, 1):
        first = (sub & bit) == 0
        merged = []
        for r in range(bit):
            kept = jnp.where(first, parts[r], parts[r + bit])
            other = jnp.where(first, parts[r + bit], parts[r])
            if bit == 4:
                moved = pltpu.roll(other, 4, 0)
            else:
                moved = jnp.where(first, pltpu.roll(other, 8 - bit, 0), pltpu.roll(other, bit, 0))
            merged.append(kept + moved)
        parts = merged
    return parts[0]


def branch_sums(read):
    total = jnp.zeros((8, 128), F32)
    for k8 in range(KS // 8):
        total = total + read(slice(k8 * 8, k8 * 8 + 8))
    return total


def weigh_kernel(counts_hbm, totals_hbm, lengths_hbm, wt_ref, split_ref, col_ref, *scratch):
    counts_ref, totals_ref, lengths_ref, sems = scratch
    loads = [
        pltpu.make_async_copy(src, dst, sems.at[n])
        for n, (src, dst) in enumerate(
            ((counts_hbm, counts_ref), (totals_hbm, totals_ref), (lengths_hbm, lengths_ref))
        )
    ]
    for load in loads:
        load.start()
    for load in loads:
        load.wait()
    scaled = lengths_ref[...].astype(F32) * 0.001
    wt = (scaled * counts_ref[...].astype(F32)).T / totals_ref[...].astype(F32)
    wt_ref[...] = wt
    for n in range(8):
        x = wt[:, n * 32 : (n + 1) * 32]
        high = x.astype(BF16)
        rest = x - high.astype(F32)
        middle = rest.astype(BF16)
        low = (rest - middle.astype(F32)).astype(BF16)
        split_ref[n] = jnp.concatenate([high, middle, low, jnp.zeros_like(low)], axis=1)
    sums = row_sums(
        [branch_sums(lambda at, h=h: wt_ref[at, h * 128 : h * 128 + 128]) for h in range(2)]
    )
    for h in range(2):
        col_ref[h * 128 : (h + 1) * 128, :] = jnp.broadcast_to(sums[h : h + 1], (128, 128)).T


def weigh(counts, totals, lengths):
    return pl.pallas_call(
        weigh_kernel,
        out_shape=(
            jax.ShapeDtypeStruct((KS, ROWS), F32),
            jax.ShapeDtypeStruct((8, KS, 128), BF16),
            jax.ShapeDtypeStruct((ROWS, 128), F32),
        ),
        in_specs=[pl.BlockSpec(memory_space=pltpu.HBM)] * 3,
        out_specs=tuple(in_vmem(3)),
        scratch_shapes=[
            pltpu.VMEM((ROWS, KS), jnp.int32),
            pltpu.VMEM((1, ROWS), jnp.int32),
            pltpu.VMEM((1, KS), jnp.int32),
            pltpu.SemaphoreType.DMA((3,)),
        ],
        compiler_params=params(),
        name="weigh",
    )(counts, totals.reshape(1, ROWS), lengths.reshape(1, KS))


def spread_call(name, n_blocks, columns, width, group, mass_row, side=None):
    pairs = group // 2
    halves = 2 if side is None else 1
    groups = halves * ROWS // 2 // group

    def kernel(split_ref, col_ref, *refs):
        blocks = refs[:n_blocks]
        out_ref, pick_ref, even_ref, odd_ref = refs[n_blocks:]
        core = lax.axis_index("branch") % 2
        y = lax.axis_index("blk") // 4
        if side is None:
            base = 0
        else:
            base = (core if side == 0 else 1 - core) * groups

        part = lax.broadcasted_iota(jnp.int32, (128, 256), 0)
        lane = lax.broadcasted_iota(jnp.int32, (128, 256), 1)
        want = jnp.where(part < 96, part % 32 - lane // 128, -1)
        for p in range(16):
            pick_ref[p] = jnp.where(want == 2 * p, 1.0, 0.0).astype(BF16)

        def broadcast_pair(into, g, q, at=slice(0, KS)):
            pair = g * pairs + q
            into[q, at] = jnp.dot(
                split_ref[pair // 16, at], pick_ref[pair % 16], preferred_element_type=F32
            )

        def span(n, lane, at):
            if isinstance(lane, int):
                return blocks[n][at, lane : lane + 128]
            return blocks[n][at, pl.ds(pl.multiple_of(lane, 128), 128)]

        def columns_at(h):
            return columns(h if side is None else base // groups, y)

        for h in range(halves):
            totals = [
                branch_sums(lambda at, n=n, lane=lane: span(n, lane, at))
                for n, lane in columns_at(h)
            ]
            masses = row_sums([jnp.zeros((8, 128), F32)] * mass_row + totals)
            out_ref[h, 128:136, 0:128] = masses

        for q in range(pairs):
            broadcast_pair(even_ref, base, q)

        def one_group(g, now, later):
            h = g * group // 128
            cols = columns_at(h)
            n_cols = len(cols)
            following = base + jnp.minimum(g + 1, groups - 1)
            steps = []
            if group == 8:
                for q in range(pairs):
                    broadcast_pair(later, following, q)
            else:
                steps = [(q, slice(k, k + 128)) for k in range(0, KS, 128) for q in range(pairs)]
            acc = [jnp.zeros((8, 128), F32)] * (group * n_cols)
            for k8 in range(KS // 8):
                if steps and k8 % 2 == 0:
                    q, at = steps[k8 // 2]
                    broadcast_pair(later, following, q, at)
                at = slice(k8 * 8, k8 * 8 + 8)
                spans = [span(n, lane, at) for n, lane in cols]
                for r in range(group):
                    own = now[r // 2, at, 128 * (r % 2) : 128 * (r % 2) + 128]
                    for j in range(n_cols):
                        acc[r * n_cols + j] += jnp.minimum(own, spans[j])
            for r0 in range(0, group, 8):
                row = pl.multiple_of(g * group + r0 - h * 128, 8)
                first = pl.multiple_of((base + g) * group + r0, 8)
                own_mass = col_ref[pl.ds(first, 8), :]
                for j in range(n_cols):
                    mass = out_ref[h, 128 + mass_row + j : 129 + mass_row + j, 0:128]
                    least = row_sums([acc[(r0 + r) * n_cols + j] for r in range(8)])
                    out_ref[h, pl.ds(row, 8), 128 * j : 128 * j + 128] = (
                        own_mass + mass - 2.0 * least
                    )

        def two_groups(t, carry):
            one_group(2 * t, even_ref, odd_ref)
            one_group(2 * t + 1, odd_ref, even_ref)
            return carry

        lax.fori_loop(0, groups // 2, two_groups, 0)

    def call(split, col, *blocks):
        return pl.pallas_call(
            kernel,
            out_shape=jax.ShapeDtypeStruct((halves, 136, width), F32),
            in_specs=in_vmem(2 + n_blocks),
            out_specs=in_vmem(1)[0],
            scratch_shapes=[
                pltpu.VMEM((16, 128, 256), BF16),
                pltpu.VMEM((pairs, KS, 256), F32),
                pltpu.VMEM((pairs, KS, 256), F32),
            ],
            compiler_params=params(),
            cost_estimate=pl.CostEstimate(
                flops=halves * width * 128 * KS * 250, bytes_accessed=4 << 20, transcendentals=0
            ),
            name=name,
        )(split, col, *blocks)

    return call


def diagonal_columns(half, y):
    return [(0, 0), (0, 128)]


def first_columns(half, y):
    return [(0, 0), (0, 128), (1, 0), (1, 128)]


def second_columns(half, y):
    return [(0, 0), (0, 128), (1, (half ^ y) * 128)]


DIRECT = 1152


def pack_kernel(own0, got0, own1, got1, own2, got2, out_ref):
    core = lax.axis_index("branch") % 2
    lane = 0
    masses = []
    for own, got in ((own0, got0), (own1, got1), (own2, got2)):
        half = core if own.shape[0] == 2 else 0
        width = own.shape[2]
        both = own[half, 0:128, :] + got[half, 0:128, :]
        out_ref[:, :, lane : lane + width] = both.reshape(16, 8, width)
        masses.append(own[half, 128:136, 0:128] + got[half, 128:136, 0:128])
        lane += width
    for block in (masses[0] + masses[1], masses[2]):
        out_ref[:, :, lane : lane + 128] = jnp.broadcast_to(block[None], (16, 8, 128))
        lane += 128


def pack(*parts):
    return pl.pallas_call(
        pack_kernel,
        out_shape=jax.ShapeDtypeStruct((16, 8, DIRECT + 256), F32),
        in_specs=in_vmem(6),
        out_specs=in_vmem(1)[0],
        compiler_params=params(),
        name="pack",
    )(*parts)


def block_partner(b, slot):
    y, x = b // 4, b % 4
    if slot == 0:
        return b
    if slot == 1:
        return y * 4 + (x + 1) % 4
    if slot == 2:
        return (1 - y) * 4 + (x + 3) % 4
    if slot == 4:
        return (1 - y) * 4 + (x + 2) % 4
    if slot == 5:
        return y * 4 + (x + 3) % 4
    if slot == 6:
        return (1 - y) * 4 + (x + 1) % 4
    far = x // 2
    keep_y = (far == y) if slot == 3 else (far != y)
    return jnp.where(keep_y, y * 4 + (x + 2) % 4, (1 - y) * 4 + x)


def normalise_kernel(shards_ref, out_ref):
    branch = lax.axis_index("branch")
    core, place = branch % 2, branch // 2
    total = jnp.sum(shards_ref[...], axis=0)
    rows = [total[r : r + 1, DIRECT : DIRECT + 128] for r in range(6)]
    rows += [total[r : r + 1, DIRECT + 128 : DIRECT + 256] for r in range(3)]
    mine = jnp.broadcast_to(jnp.where(core == 0, rows[0], rows[1]), (8, 128))
    lane = lax.broadcasted_iota(jnp.int32, (8, 128), 1)
    row = lax.broadcasted_iota(jnp.int32, (8, 128), 0)
    own = jnp.sum(jnp.where(lane == place * 8 + row, mine, 0.0), axis=1, keepdims=True)
    for j in range(DIRECT // 128):
        at = slice(128 * j, 128 * j + 128)
        dist = total[:, at] / (own + rows[j])
        out_ref[:, :, at] = jnp.broadcast_to(dist[None], (16, 8, 128))


def normalise(shards):
    return pl.pallas_call(
        normalise_kernel,
        out_shape=jax.ShapeDtypeStruct((16, 8, DIRECT), F32),
        in_specs=in_vmem(1),
        out_specs=in_vmem(1)[0],
        compiler_params=params(),
        name="normalise",
    )(shards)


def assemble_kernel(own, other, own_swapped, other_swapped, out_ref, turned_ref, sems):
    core = lax.axis_index("branch") % 2
    b = lax.axis_index("blk")
    y = b // 4
    stores = []

    def store(src, rows, cols):
        copy = pltpu.make_async_copy(src, out_ref.at[rows, cols], sems.at[len(stores)])
        copy.start()
        stores.append(copy)

    def rows_of(half):
        return pl.ds(pl.multiple_of(half * 128, 128), 128)

    def columns(slot, half=None):
        first = block_partner(b, slot) * ROWS
        if half is None:
            return pl.ds(pl.multiple_of(first, ROWS), ROWS)
        return pl.ds(pl.multiple_of(first + half * 128, 128), 128)

    for half, ref in ((core, own), (1 - core, other)):
        rows = rows_of(half)
        for slot in range(4):
            store(ref.at[:, slot * ROWS : (slot + 1) * ROWS], rows, columns(slot))
        store(ref.at[:, 4 * ROWS : DIRECT], rows, columns(4, half ^ y))
    for side, half, ref in ((0, core, own_swapped), (1, 1 - core, other_swapped)):
        for n, slot in enumerate((5, 6, 7)):
            turned_ref[side, n] = ref[:, n * ROWS : (n + 1) * ROWS].T
            store(turned_ref.at[side, n], slice(0, ROWS), columns(slot, half))
        turned_ref[side, 3, 0:128] = ref[:, 3 * ROWS :].T
        store(turned_ref.at[side, 3, 0:128], rows_of(half ^ (1 - y)), columns(4, half))
    for copy in stores:
        copy.wait()


def assemble(*pieces):
    return pl.pallas_call(
        assemble_kernel,
        out_shape=jax.ShapeDtypeStruct((ROWS, BLOCKS * ROWS), F32),
        in_specs=in_vmem(4),
        out_specs=pl.BlockSpec(memory_space=pl.ANY),
        scratch_shapes=[
            pltpu.VMEM((2, 4, ROWS, 128), F32),
            pltpu.SemaphoreType.DMA((18,)),
        ],
        compiler_params=params(),
        name="assemble",
    )(*pieces)


def on_device(counts, totals, lengths):
    def from_partner(v, n):
        return lax.ppermute(v, "blk", [(PARTNERS[n][b], b) for b in range(BLOCKS)])

    def other_core(v):
        return lax.ppermute(v, "branch", [(i, i ^ 1) for i in range(32)])

    chips = [[2 * p + c for p in range(16)] for c in range(2)]

    def over_chips(v):
        return lax.all_to_all(v, "branch", 0, 0, axis_index_groups=chips)

    wt, split, mass_col = weigh(counts, totals, lengths)
    got = [from_partner(wt, n) for n in range(2)]
    diagonal = spread_call("diagonal", 1, diagonal_columns, 256, 16, 0)
    first = spread_call("first", 2, first_columns, 512, 8, 2)
    second = [spread_call(f"second{s}", 2, second_columns, 384, 8, 0, s) for s in range(2)]

    part0 = diagonal(split, mass_col, wt)
    later = lax.optimization_barrier((wt, part0))[0]
    got += [from_partner(later, n) for n in (2, 3)]
    received0 = other_core(part0)
    part1 = first(split, mass_col, got[0], got[1])
    received1 = other_core(part1)
    third = lax.optimization_barrier((got[2], part1))[0]
    sent2 = second[1](split, mass_col, third, got[3])
    received2 = other_core(sent2)
    third = lax.optimization_barrier((third, sent2))[0]
    part2 = second[0](split, mass_col, third, got[3])

    shards = over_chips(pack(part0, received0, part1, received1, part2, received2))
    own = over_chips(normalise(shards)).reshape(128, DIRECT)
    swapped = []
    for n in range(4):
        tile = own[:, (n + 1) * ROWS : min((n + 2) * ROWS, DIRECT)]
        swapped.append(lax.ppermute(tile, "blk", [(b, PARTNERS[n][b]) for b in range(BLOCKS)]))
    other = other_core(own)
    swapped = jnp.concatenate(swapped, axis=1)
    return assemble(own, other, swapped, other_core(swapped))


def solution(mesh):
    placed = (P("blk", "branch"), P("blk"), P("branch"))
    return jax.shard_map(
        on_device, mesh=mesh, in_specs=placed, out_specs=P("blk", None), check_vma=False
    )
```

```python
import jax
import jax.numpy as jnp
from jax import lax
from jax.experimental import pallas as pl
from jax.experimental.pallas import tpu as pltpu
from jax.sharding import PartitionSpec as P

F32 = jnp.float32
BF16 = jnp.bfloat16
ROWS = 256
KS = 512
BLOCKS = 8
GROUP = 8
PAIRS = GROUP // 2
GROUPS = ROWS // GROUP


def block_at(y, x):
    return (y % 2) * 4 + x % 4


def partner_tables():
    first, second, third, fourth = [], [], [], []
    for b in range(BLOCKS):
        y, x = b // 4, b % 4
        first.append(block_at(y, x + 1))
        second.append(block_at(y + 1, x + 3))
        cycle = {(0, 0): (0, 2), (0, 1): (1, 2), (1, 1): (1, 0), (1, 0): (0, 0)}
        ny, nx = cycle[(y, x // 2)]
        third.append(block_at(ny, nx + x % 2))
        fourth.append(block_at(y + 1, x + 2))
    return [first, second, third, fourth]


PARTNERS = partner_tables()


def params():
    return pltpu.CompilerParams(vmem_limit_bytes=24 << 20)


def in_vmem(n):
    return [pl.BlockSpec(memory_space=pltpu.VMEM)] * n


def row_sums(parts):
    parts = parts + [jnp.zeros((8, 128), F32)] * (8 - len(parts))
    sub = lax.broadcasted_iota(jnp.int32, (8, 128), 0)
    for bit in (4, 2, 1):
        first = (sub & bit) == 0
        merged = []
        for r in range(bit):
            kept = jnp.where(first, parts[r], parts[r + bit])
            other = jnp.where(first, parts[r + bit], parts[r])
            if bit == 4:
                moved = pltpu.roll(other, 4, 0)
            else:
                moved = jnp.where(first, pltpu.roll(other, 8 - bit, 0), pltpu.roll(other, bit, 0))
            merged.append(kept + moved)
        parts = merged
    return parts[0]


def branch_sums(read):
    total = jnp.zeros((8, 128), F32)
    for k8 in range(KS // 8):
        total = total + read(slice(k8 * 8, k8 * 8 + 8))
    return total


def weigh_kernel(counts_hbm, totals_hbm, lengths_hbm, wt_ref, split_ref, col_ref, *scratch):
    counts_ref, totals_ref, lengths_ref, sems = scratch
    loads = [
        pltpu.make_async_copy(src, dst, sems.at[n])
        for n, (src, dst) in enumerate(
            ((counts_hbm, counts_ref), (totals_hbm, totals_ref), (lengths_hbm, lengths_ref))
        )
    ]
    for load in loads:
        load.start()
    for load in loads:
        load.wait()
    scaled = lengths_ref[...].astype(F32) * 0.001
    wt = (scaled * counts_ref[...].astype(F32)).T / totals_ref[...].astype(F32)
    wt_ref[...] = wt
    for n in range(8):
        x = wt[:, n * 32 : (n + 1) * 32]
        high = x.astype(BF16)
        rest = x - high.astype(F32)
        middle = rest.astype(BF16)
        low = (rest - middle.astype(F32)).astype(BF16)
        split_ref[n] = jnp.concatenate([high, middle, low, jnp.zeros_like(low)], axis=1)
    sums = row_sums(
        [branch_sums(lambda at, h=h: wt_ref[at, h * 128 : h * 128 + 128]) for h in range(2)]
    )
    for h in range(2):
        col_ref[h * 128 : (h + 1) * 128, :] = jnp.broadcast_to(sums[h : h + 1], (128, 128)).T


def weigh(counts, totals, lengths):
    return pl.pallas_call(
        weigh_kernel,
        out_shape=(
            jax.ShapeDtypeStruct((KS, ROWS), F32),
            jax.ShapeDtypeStruct((8, KS, 128), BF16),
            jax.ShapeDtypeStruct((ROWS, 128), F32),
        ),
        in_specs=[pl.BlockSpec(memory_space=pltpu.HBM)] * 3,
        out_specs=tuple(in_vmem(3)),
        scratch_shapes=[
            pltpu.VMEM((ROWS, KS), jnp.int32),
            pltpu.VMEM((1, ROWS), jnp.int32),
            pltpu.VMEM((1, KS), jnp.int32),
            pltpu.SemaphoreType.DMA((3,)),
        ],
        compiler_params=params(),
        name="weigh",
    )(counts, totals.reshape(1, ROWS), lengths.reshape(1, KS))


def spread_call(name, n_blocks, columns, width, group, mass_row, side=None):
    pairs = group // 2
    halves = 2 if side is None else 1
    groups = halves * ROWS // 2 // group

    def kernel(split_ref, col_ref, *refs):
        blocks = refs[:n_blocks]
        out_ref, pick_ref, even_ref, odd_ref = refs[n_blocks:]
        core = lax.axis_index("branch") % 2
        y = lax.axis_index("blk") // 4
        if side is None:
            base = 0
        else:
            base = (core if side == 0 else 1 - core) * groups

        part = lax.broadcasted_iota(jnp.int32, (128, 256), 0)
        lane = lax.broadcasted_iota(jnp.int32, (128, 256), 1)
        want = jnp.where(part < 96, part % 32 - lane // 128, -1)
        for p in range(16):
            pick_ref[p] = jnp.where(want == 2 * p, 1.0, 0.0).astype(BF16)

        def broadcast_pair(into, g, q, at=slice(0, KS)):
            pair = g * pairs + q
            into[q, at] = jnp.dot(
                split_ref[pair // 16, at], pick_ref[pair % 16], preferred_element_type=F32
            )

        def span(n, lane, at):
            if isinstance(lane, int):
                return blocks[n][at, lane : lane + 128]
            return blocks[n][at, pl.ds(pl.multiple_of(lane, 128), 128)]

        def columns_at(h):
            return columns(h if side is None else base // groups, y)

        for h in range(halves):
            totals = [
                branch_sums(lambda at, n=n, lane=lane: span(n, lane, at))
                for n, lane in columns_at(h)
            ]
            masses = row_sums([jnp.zeros((8, 128), F32)] * mass_row + totals)
            out_ref[h, 128:136, 0:128] = masses

        for q in range(pairs):
            broadcast_pair(even_ref, base, q)

        def one_group(g, now, later):
            h = g * group // 128
            cols = columns_at(h)
            n_cols = len(cols)
            following = base + jnp.minimum(g + 1, groups - 1)
            for q in range(pairs):
                broadcast_pair(later, following, q)
            acc = [jnp.zeros((8, 128), F32)] * (group * n_cols)
            for k8 in range(KS // 8):
                at = slice(k8 * 8, k8 * 8 + 8)
                spans = [span(n, lane, at) for n, lane in cols]
                for r in range(group):
                    own = now[r // 2, at, 128 * (r % 2) : 128 * (r % 2) + 128]
                    for j in range(n_cols):
                        acc[r * n_cols + j] += jnp.minimum(own, spans[j])
            for r0 in range(0, group, 8):
                row = pl.multiple_of(g * group + r0 - h * 128, 8)
                first = pl.multiple_of((base + g) * group + r0, 8)
                own_mass = col_ref[pl.ds(first, 8), :]
                for j in range(n_cols):
                    mass = out_ref[h, 128 + mass_row + j : 129 + mass_row + j, 0:128]
                    least = row_sums([acc[(r0 + r) * n_cols + j] for r in range(8)])
                    out_ref[h, pl.ds(row, 8), 128 * j : 128 * j + 128] = (
                        own_mass + mass - 2.0 * least
                    )

        def two_groups(t, carry):
            one_group(2 * t, even_ref, odd_ref)
            one_group(2 * t + 1, odd_ref, even_ref)
            return carry

        lax.fori_loop(0, groups // 2, two_groups, 0)

    def call(split, col, *blocks):
        return pl.pallas_call(
            kernel,
            out_shape=jax.ShapeDtypeStruct((halves, 136, width), F32),
            in_specs=in_vmem(2 + n_blocks),
            out_specs=in_vmem(1)[0],
            scratch_shapes=[
                pltpu.VMEM((16, 128, 256), BF16),
                pltpu.VMEM((pairs, KS, 256), F32),
                pltpu.VMEM((pairs, KS, 256), F32),
            ],
            compiler_params=params(),
            cost_estimate=pl.CostEstimate(
                flops=halves * width * 128 * KS * 250, bytes_accessed=4 << 20, transcendentals=0
            ),
            name=name,
        )(split, col, *blocks)

    return call


def diagonal_columns(half, y):
    return [(0, 0), (0, 128)]


def first_columns(half, y):
    return [(0, 0), (0, 128), (1, 0), (1, 128)]


def second_columns(half, y):
    return [(0, 0), (0, 128), (1, (half ^ y) * 128)]


DIRECT = 1152


def pack_kernel(own0, got0, own1, got1, own2, got2, out_ref):
    core = lax.axis_index("branch") % 2
    lane = 0
    masses = []
    for own, got in ((own0, got0), (own1, got1), (own2, got2)):
        half = core if own.shape[0] == 2 else 0
        width = own.shape[2]
        both = own[half, 0:128, :] + got[half, 0:128, :]
        out_ref[:, :, lane : lane + width] = both.reshape(16, 8, width)
        masses.append(own[half, 128:136, 0:128] + got[half, 128:136, 0:128])
        lane += width
    for block in (masses[0] + masses[1], masses[2]):
        out_ref[:, :, lane : lane + 128] = jnp.broadcast_to(block[None], (16, 8, 128))
        lane += 128


def pack(*parts):
    return pl.pallas_call(
        pack_kernel,
        out_shape=jax.ShapeDtypeStruct((16, 8, DIRECT + 256), F32),
        in_specs=in_vmem(6),
        out_specs=in_vmem(1)[0],
        compiler_params=params(),
        name="pack",
    )(*parts)


def block_partner(b, slot):
    y, x = b // 4, b % 4
    if slot == 0:
        return b
    if slot == 1:
        return y * 4 + (x + 1) % 4
    if slot == 2:
        return (1 - y) * 4 + (x + 3) % 4
    if slot == 4:
        return (1 - y) * 4 + (x + 2) % 4
    if slot == 5:
        return y * 4 + (x + 3) % 4
    if slot == 6:
        return (1 - y) * 4 + (x + 1) % 4
    far = x // 2
    keep_y = (far == y) if slot == 3 else (far != y)
    return jnp.where(keep_y, y * 4 + (x + 2) % 4, (1 - y) * 4 + x)


def normalise_kernel(shards_ref, out_ref):
    branch = lax.axis_index("branch")
    core, place = branch % 2, branch // 2
    total = jnp.sum(shards_ref[...], axis=0)
    rows = [total[r : r + 1, DIRECT : DIRECT + 128] for r in range(6)]
    rows += [total[r : r + 1, DIRECT + 128 : DIRECT + 256] for r in range(3)]
    mine = jnp.broadcast_to(jnp.where(core == 0, rows[0], rows[1]), (8, 128))
    lane = lax.broadcasted_iota(jnp.int32, (8, 128), 1)
    row = lax.broadcasted_iota(jnp.int32, (8, 128), 0)
    own = jnp.sum(jnp.where(lane == place * 8 + row, mine, 0.0), axis=1, keepdims=True)
    for j in range(DIRECT // 128):
        at = slice(128 * j, 128 * j + 128)
        dist = total[:, at] / (own + rows[j])
        out_ref[:, :, at] = jnp.broadcast_to(dist[None], (16, 8, 128))


def normalise(shards):
    return pl.pallas_call(
        normalise_kernel,
        out_shape=jax.ShapeDtypeStruct((16, 8, DIRECT), F32),
        in_specs=in_vmem(1),
        out_specs=in_vmem(1)[0],
        compiler_params=params(),
        name="normalise",
    )(shards)


def assemble_kernel(own, other, own_swapped, other_swapped, out_ref, turned_ref, sems):
    core = lax.axis_index("branch") % 2
    b = lax.axis_index("blk")
    y = b // 4
    stores = []

    def store(src, rows, cols):
        copy = pltpu.make_async_copy(src, out_ref.at[rows, cols], sems.at[len(stores)])
        copy.start()
        stores.append(copy)

    def rows_of(half):
        return pl.ds(pl.multiple_of(half * 128, 128), 128)

    def columns(slot, half=None):
        first = block_partner(b, slot) * ROWS
        if half is None:
            return pl.ds(pl.multiple_of(first, ROWS), ROWS)
        return pl.ds(pl.multiple_of(first + half * 128, 128), 128)

    for half, ref in ((core, own), (1 - core, other)):
        rows = rows_of(half)
        for slot in range(4):
            store(ref.at[:, slot * ROWS : (slot + 1) * ROWS], rows, columns(slot))
        store(ref.at[:, 4 * ROWS : DIRECT], rows, columns(4, half ^ y))
    for side, half, ref in ((0, core, own_swapped), (1, 1 - core, other_swapped)):
        for n, slot in enumerate((5, 6, 7)):
            turned_ref[side, n] = ref[:, n * ROWS : (n + 1) * ROWS].T
            store(turned_ref.at[side, n], slice(0, ROWS), columns(slot, half))
        turned_ref[side, 3, 0:128] = ref[:, 3 * ROWS :].T
        store(turned_ref.at[side, 3, 0:128], rows_of(half ^ (1 - y)), columns(4, half))
    for copy in stores:
        copy.wait()


def assemble(*pieces):
    return pl.pallas_call(
        assemble_kernel,
        out_shape=jax.ShapeDtypeStruct((ROWS, BLOCKS * ROWS), F32),
        in_specs=in_vmem(4),
        out_specs=pl.BlockSpec(memory_space=pl.ANY),
        scratch_shapes=[
            pltpu.VMEM((2, 4, ROWS, 128), F32),
            pltpu.SemaphoreType.DMA((18,)),
        ],
        compiler_params=params(),
        name="assemble",
    )(*pieces)


def on_device(counts, totals, lengths):
    def from_partner(v, n):
        return lax.ppermute(v, "blk", [(PARTNERS[n][b], b) for b in range(BLOCKS)])

    def other_core(v):
        return lax.ppermute(v, "branch", [(i, i ^ 1) for i in range(32)])

    chips = [[2 * p + c for p in range(16)] for c in range(2)]

    def over_chips(v):
        return lax.all_to_all(v, "branch", 0, 0, axis_index_groups=chips)

    wt, split, mass_col = weigh(counts, totals, lengths)
    got = [from_partner(wt, n) for n in range(2)]
    diagonal = spread_call("diagonal", 1, diagonal_columns, 256, 16, 0)
    first = spread_call("first", 2, first_columns, 512, 16, 2)
    second = [spread_call(f"second{s}", 2, second_columns, 384, 16, 0, s) for s in range(2)]

    part0 = diagonal(split, mass_col, wt)
    later = lax.optimization_barrier((wt, part0))[0]
    got += [from_partner(later, n) for n in (2, 3)]
    part1 = first(split, mass_col, got[0], got[1])
    received0 = other_core(lax.optimization_barrier((part0, part1))[0])
    received1 = other_core(part1)
    third = lax.optimization_barrier((got[2], part1))[0]
    sent2 = second[1](split, mass_col, third, got[3])
    received2 = other_core(sent2)
    third = lax.optimization_barrier((third, sent2))[0]
    part2 = second[0](split, mass_col, third, got[3])

    shards = over_chips(pack(part0, received0, part1, received1, part2, received2))
    own = over_chips(normalise(shards)).reshape(128, DIRECT)
    swapped = []
    for n in range(4):
        tile = own[:, (n + 1) * ROWS : min((n + 2) * ROWS, DIRECT)]
        swapped.append(lax.ppermute(tile, "blk", [(b, PARTNERS[n][b]) for b in range(BLOCKS)]))
    other = other_core(own)
    swapped = jnp.concatenate(swapped, axis=1)
    return assemble(own, other, swapped, other_core(swapped))


def solution(mesh):
    placed = (P("blk", "branch"), P("blk"), P("branch"))
    return jax.shard_map(
        on_device, mesh=mesh, in_specs=placed, out_specs=P("blk", None), check_vma=False
    )
```

```python
import jax
import jax.numpy as jnp
from jax import lax
from jax.experimental import pallas as pl
from jax.experimental.pallas import tpu as pltpu
from jax.sharding import PartitionSpec as P

F32 = jnp.float32
BF16 = jnp.bfloat16
ROWS = 256
KS = 512
BLOCKS = 8
GROUP = 8
PAIRS = GROUP // 2
GROUPS = ROWS // GROUP


def block_at(y, x):
    return (y % 2) * 4 + x % 4


def partner_tables():
    first, second, third, fourth = [], [], [], []
    for b in range(BLOCKS):
        y, x = b // 4, b % 4
        first.append(block_at(y, x + 1))
        second.append(block_at(y + 1, x + 3))
        cycle = {(0, 0): (0, 2), (0, 1): (1, 2), (1, 1): (1, 0), (1, 0): (0, 0)}
        ny, nx = cycle[(y, x // 2)]
        third.append(block_at(ny, nx + x % 2))
        fourth.append(block_at(y + 1, x + 2))
    return [first, second, third, fourth]


PARTNERS = partner_tables()


def params():
    return pltpu.CompilerParams(vmem_limit_bytes=24 << 20)


def in_vmem(n):
    return [pl.BlockSpec(memory_space=pltpu.VMEM)] * n


def row_sums(parts):
    parts = parts + [jnp.zeros((8, 128), F32)] * (8 - len(parts))
    sub = lax.broadcasted_iota(jnp.int32, (8, 128), 0)
    for bit in (4, 2, 1):
        first = (sub & bit) == 0
        merged = []
        for r in range(bit):
            kept = jnp.where(first, parts[r], parts[r + bit])
            other = jnp.where(first, parts[r + bit], parts[r])
            if bit == 4:
                moved = pltpu.roll(other, 4, 0)
            else:
                moved = jnp.where(first, pltpu.roll(other, 8 - bit, 0), pltpu.roll(other, bit, 0))
            merged.append(kept + moved)
        parts = merged
    return parts[0]


def branch_sums(read):
    total = jnp.zeros((8, 128), F32)
    for k8 in range(KS // 8):
        total = total + read(slice(k8 * 8, k8 * 8 + 8))
    return total


def weigh_kernel(counts_hbm, totals_hbm, lengths_hbm, wt_ref, split_ref, col_ref, *scratch):
    counts_ref, totals_ref, lengths_ref, sems = scratch
    loads = [
        pltpu.make_async_copy(src, dst, sems.at[n])
        for n, (src, dst) in enumerate(
            ((counts_hbm, counts_ref), (totals_hbm, totals_ref), (lengths_hbm, lengths_ref))
        )
    ]
    for load in loads:
        load.start()
    for load in loads:
        load.wait()
    scaled = lengths_ref[...].astype(F32) * 0.001
    wt = (scaled * counts_ref[...].astype(F32)).T / totals_ref[...].astype(F32)
    wt_ref[...] = wt
    for n in range(8):
        x = wt[:, n * 32 : (n + 1) * 32]
        high = x.astype(BF16)
        rest = x - high.astype(F32)
        middle = rest.astype(BF16)
        low = (rest - middle.astype(F32)).astype(BF16)
        split_ref[n] = jnp.concatenate([high, middle, low, jnp.zeros_like(low)], axis=1)
    sums = row_sums(
        [branch_sums(lambda at, h=h: wt_ref[at, h * 128 : h * 128 + 128]) for h in range(2)]
    )
    for h in range(2):
        col_ref[h * 128 : (h + 1) * 128, :] = jnp.broadcast_to(sums[h : h + 1], (128, 128)).T


def weigh(counts, totals, lengths):
    return pl.pallas_call(
        weigh_kernel,
        out_shape=(
            jax.ShapeDtypeStruct((KS, ROWS), F32),
            jax.ShapeDtypeStruct((8, KS, 128), BF16),
            jax.ShapeDtypeStruct((ROWS, 128), F32),
        ),
        in_specs=[pl.BlockSpec(memory_space=pltpu.HBM)] * 3,
        out_specs=tuple(in_vmem(3)),
        scratch_shapes=[
            pltpu.VMEM((ROWS, KS), jnp.int32),
            pltpu.VMEM((1, ROWS), jnp.int32),
            pltpu.VMEM((1, KS), jnp.int32),
            pltpu.SemaphoreType.DMA((3,)),
        ],
        compiler_params=params(),
        name="weigh",
    )(counts, totals.reshape(1, ROWS), lengths.reshape(1, KS))


def spread_call(name, n_blocks, columns, width, group, mass_row, side=None):
    pairs = group // 2
    halves = 2 if side is None else 1
    groups = halves * ROWS // 2 // group

    def kernel(split_ref, col_ref, *refs):
        blocks = refs[:n_blocks]
        out_ref, pick_ref, even_ref, odd_ref = refs[n_blocks:]
        core = lax.axis_index("branch") % 2
        y = lax.axis_index("blk") // 4
        if side is None:
            base = 0
        else:
            base = (core if side == 0 else 1 - core) * groups

        part = lax.broadcasted_iota(jnp.int32, (128, 256), 0)
        lane = lax.broadcasted_iota(jnp.int32, (128, 256), 1)
        want = jnp.where(part < 96, part % 32 - lane // 128, -1)
        for p in range(16):
            pick_ref[p] = jnp.where(want == 2 * p, 1.0, 0.0).astype(BF16)

        def broadcast_pair(into, g, q, at=slice(0, KS)):
            pair = g * pairs + q
            into[q, at] = jnp.dot(
                split_ref[pair // 16, at], pick_ref[pair % 16], preferred_element_type=F32
            )

        def span(n, lane, at):
            if isinstance(lane, int):
                return blocks[n][at, lane : lane + 128]
            return blocks[n][at, pl.ds(pl.multiple_of(lane, 128), 128)]

        def columns_at(h):
            return columns(h if side is None else base // groups, y)

        for h in range(halves):
            totals = [
                branch_sums(lambda at, n=n, lane=lane: span(n, lane, at))
                for n, lane in columns_at(h)
            ]
            masses = row_sums([jnp.zeros((8, 128), F32)] * mass_row + totals)
            out_ref[h, 128:136, 0:128] = masses

        for q in range(pairs):
            broadcast_pair(even_ref, base, q)

        def one_group(g, now, later):
            h = g * group // 128
            cols = columns_at(h)
            n_cols = len(cols)
            following = base + jnp.minimum(g + 1, groups - 1)
            for q in range(pairs):
                broadcast_pair(later, following, q)
            acc = [jnp.zeros((8, 128), F32)] * (group * n_cols)
            for k8 in range(KS // 8):
                at = slice(k8 * 8, k8 * 8 + 8)
                spans = [span(n, lane, at) for n, lane in cols]
                for r in range(group):
                    own = now[r // 2, at, 128 * (r % 2) : 128 * (r % 2) + 128]
                    for j in range(n_cols):
                        acc[r * n_cols + j] += jnp.minimum(own, spans[j])
            for r0 in range(0, group, 8):
                row = pl.multiple_of(g * group + r0 - h * 128, 8)
                first = pl.multiple_of((base + g) * group + r0, 8)
                own_mass = col_ref[pl.ds(first, 8), :]
                for j in range(n_cols):
                    mass = out_ref[h, 128 + mass_row + j : 129 + mass_row + j, 0:128]
                    least = row_sums([acc[(r0 + r) * n_cols + j] for r in range(8)])
                    out_ref[h, pl.ds(row, 8), 128 * j : 128 * j + 128] = (
                        own_mass + mass - 2.0 * least
                    )

        def two_groups(t, carry):
            one_group(2 * t, even_ref, odd_ref)
            one_group(2 * t + 1, odd_ref, even_ref)
            return carry

        lax.fori_loop(0, groups // 2, two_groups, 0)

    def call(split, col, *blocks):
        return pl.pallas_call(
            kernel,
            out_shape=jax.ShapeDtypeStruct((halves, 136, width), F32),
            in_specs=in_vmem(2 + n_blocks),
            out_specs=in_vmem(1)[0],
            scratch_shapes=[
                pltpu.VMEM((16, 128, 256), BF16),
                pltpu.VMEM((pairs, KS, 256), F32),
                pltpu.VMEM((pairs, KS, 256), F32),
            ],
            compiler_params=params(),
            cost_estimate=pl.CostEstimate(
                flops=halves * width * 128 * KS * 250, bytes_accessed=4 << 20, transcendentals=0
            ),
            name=name,
        )(split, col, *blocks)

    return call


def diagonal_columns(half, y):
    return [(0, 0), (0, 128)]


def first_columns(half, y):
    return [(0, 0), (0, 128), (1, 0), (1, 128)]


def second_columns(half, y):
    return [(0, 0), (0, 128), (1, (half ^ y) * 128)]


DIRECT = 1152


def pack_kernel(own0, got0, own1, got1, own2, got2, out_ref):
    core = lax.axis_index("branch") % 2
    lane = 0
    masses = []
    for own, got in ((own0, got0), (own1, got1), (own2, got2)):
        half = core if own.shape[0] == 2 else 0
        width = own.shape[2]
        both = own[half, 0:128, :] + got[half, 0:128, :]
        out_ref[:, :, lane : lane + width] = both.reshape(16, 8, width)
        masses.append(own[half, 128:136, 0:128] + got[half, 128:136, 0:128])
        lane += width
    for block in (masses[0] + masses[1], masses[2]):
        out_ref[:, :, lane : lane + 128] = jnp.broadcast_to(block[None], (16, 8, 128))
        lane += 128


def pack(*parts):
    return pl.pallas_call(
        pack_kernel,
        out_shape=jax.ShapeDtypeStruct((16, 8, DIRECT + 256), F32),
        in_specs=in_vmem(6),
        out_specs=in_vmem(1)[0],
        compiler_params=params(),
        name="pack",
    )(*parts)


def block_partner(b, slot):
    y, x = b // 4, b % 4
    if slot == 0:
        return b
    if slot == 1:
        return y * 4 + (x + 1) % 4
    if slot == 2:
        return (1 - y) * 4 + (x + 3) % 4
    if slot == 4:
        return (1 - y) * 4 + (x + 2) % 4
    if slot == 5:
        return y * 4 + (x + 3) % 4
    if slot == 6:
        return (1 - y) * 4 + (x + 1) % 4
    far = x // 2
    keep_y = (far == y) if slot == 3 else (far != y)
    return jnp.where(keep_y, y * 4 + (x + 2) % 4, (1 - y) * 4 + x)


def normalise_kernel(shards_ref, out_ref):
    branch = lax.axis_index("branch")
    core, place = branch % 2, branch // 2
    total = jnp.sum(shards_ref[...], axis=0)
    rows = [total[r : r + 1, DIRECT : DIRECT + 128] for r in range(6)]
    rows += [total[r : r + 1, DIRECT + 128 : DIRECT + 256] for r in range(3)]
    mine = jnp.broadcast_to(jnp.where(core == 0, rows[0], rows[1]), (8, 128))
    lane = lax.broadcasted_iota(jnp.int32, (8, 128), 1)
    row = lax.broadcasted_iota(jnp.int32, (8, 128), 0)
    own = jnp.sum(jnp.where(lane == place * 8 + row, mine, 0.0), axis=1, keepdims=True)
    for j in range(DIRECT // 128):
        at = slice(128 * j, 128 * j + 128)
        dist = total[:, at] / (own + rows[j])
        out_ref[:, :, at] = jnp.broadcast_to(dist[None], (16, 8, 128))


def normalise(shards):
    return pl.pallas_call(
        normalise_kernel,
        out_shape=jax.ShapeDtypeStruct((16, 8, DIRECT), F32),
        in_specs=in_vmem(1),
        out_specs=in_vmem(1)[0],
        compiler_params=params(),
        name="normalise",
    )(shards)


def assemble_kernel(own, other, own_swapped, other_swapped, out_ref, turned_ref, sems):
    core = lax.axis_index("branch") % 2
    b = lax.axis_index("blk")
    y = b // 4
    stores = []

    def store(src, rows, cols):
        copy = pltpu.make_async_copy(src, out_ref.at[rows, cols], sems.at[len(stores)])
        copy.start()
        stores.append(copy)

    def rows_of(half):
        return pl.ds(pl.multiple_of(half * 128, 128), 128)

    def columns(slot, half=None):
        first = block_partner(b, slot) * ROWS
        if half is None:
            return pl.ds(pl.multiple_of(first, ROWS), ROWS)
        return pl.ds(pl.multiple_of(first + half * 128, 128), 128)

    for half, ref in ((core, own), (1 - core, other)):
        rows = rows_of(half)
        for slot in range(4):
            store(ref.at[:, slot * ROWS : (slot + 1) * ROWS], rows, columns(slot))
        store(ref.at[:, 4 * ROWS : DIRECT], rows, columns(4, half ^ y))
    for side, half, ref in ((0, core, own_swapped), (1, 1 - core, other_swapped)):
        for n, slot in enumerate((5, 6, 7)):
            turned_ref[side, n] = ref[:, n * ROWS : (n + 1) * ROWS].T
            store(turned_ref.at[side, n], slice(0, ROWS), columns(slot, half))
        turned_ref[side, 3, 0:128] = ref[:, 3 * ROWS :].T
        store(turned_ref.at[side, 3, 0:128], rows_of(half ^ (1 - y)), columns(4, half))
    for copy in stores:
        copy.wait()


def assemble(*pieces):
    return pl.pallas_call(
        assemble_kernel,
        out_shape=jax.ShapeDtypeStruct((ROWS, BLOCKS * ROWS), F32),
        in_specs=in_vmem(4),
        out_specs=pl.BlockSpec(memory_space=pl.ANY),
        scratch_shapes=[
            pltpu.VMEM((2, 4, ROWS, 128), F32),
            pltpu.SemaphoreType.DMA((18,)),
        ],
        compiler_params=params(),
        name="assemble",
    )(*pieces)


def on_device(counts, totals, lengths):
    def from_partner(v, n):
        return lax.ppermute(v, "blk", [(PARTNERS[n][b], b) for b in range(BLOCKS)])

    def other_core(v):
        return lax.ppermute(v, "branch", [(i, i ^ 1) for i in range(32)])

    chips = [[2 * p + c for p in range(16)] for c in range(2)]

    def over_chips(v):
        return lax.all_to_all(v, "branch", 0, 0, axis_index_groups=chips)

    wt, split, mass_col = weigh(counts, totals, lengths)
    got = [from_partner(wt, n) for n in range(2)]
    diagonal = spread_call("diagonal", 1, diagonal_columns, 256, 16, 0)
    first = spread_call("first", 2, first_columns, 512, 16, 2)
    second = [spread_call(f"second{s}", 2, second_columns, 384, 16, 0, s) for s in range(2)]

    part0 = diagonal(split, mass_col, wt)
    later = lax.optimization_barrier((wt, part0))[0]
    got += [from_partner(later, n) for n in (2, 3)]
    received0 = other_core(part0)
    part1 = first(split, mass_col, got[0], got[1])
    received1 = other_core(part1)
    third = lax.optimization_barrier((got[2], part1))[0]
    sent2 = second[1](split, mass_col, third, got[3])
    received2 = other_core(sent2)
    third = lax.optimization_barrier((third, sent2))[0]
    part2 = second[0](split, mass_col, third, got[3])

    shards = over_chips(pack(part0, received0, part1, received1, part2, received2))
    own = over_chips(normalise(shards)).reshape(128, DIRECT)
    swapped = []
    for n in range(4):
        tile = own[:, (n + 1) * ROWS : min((n + 2) * ROWS, DIRECT)]
        swapped.append(lax.ppermute(tile, "blk", [(b, PARTNERS[n][b]) for b in range(BLOCKS)]))
    other = other_core(own)
    swapped = jnp.concatenate(swapped, axis=1)
    return assemble(own, other, swapped, other_core(swapped))


def solution(mesh):
    placed = (P("blk", "branch"), P("blk"), P("branch"))
    return jax.shard_map(
        on_device, mesh=mesh, in_specs=placed, out_specs=P("blk", None), check_vma=False
    )
```
